256 devices in a mesh: pipe: 8 (over y, core), tensor: 32 (over z, x).
Axes of the slice: x: 4, y: 4, z: 8, core: 2. Of those that a mesh axis runs over, the one named last changes fastest.
Arguments:
- saved_inputs: bfloat16 [8, 4, 256, 4096], P('pipe', None, 'tensor'), may hold values from -6 to 6
- gate_weight: bfloat16 [8, 4096, 12288], P('pipe', None, 'tensor'), may hold values from -0.09375 to 0.09375
- up_weight: bfloat16 [8, 4096, 12288], P('pipe', None, 'tensor'), may hold values from -0.09375 to 0.09375
- down_weight: bfloat16 [8, 12288, 4096], P('pipe', 'tensor'), may hold values from -0.0546875 to 0.0546875
- section_grads: bfloat16 [8, 256, 4096], P('pipe', 'tensor'), may hold values from -6 to 6
- loss_grad: bfloat16 [256, 4096], P('tensor'), may hold values from -6 to 6
- trainable: int32 [1], replicated, may hold values from 0 to 511
- slot_table: int32 [2, 8], replicated, may hold values from 0 to 3, as said below
Outputs:
- input_grads: bfloat16 [2, 8, 256, 4096], P(None, 'pipe', 'tensor')
- grad_gate: bfloat16 [4096, 12288], P('pipe', 'tensor')
- grad_up: bfloat16 [4096, 12288], P('pipe', 'tensor')
- grad_down: bfloat16 [12288, 4096], P('tensor', 'pipe')
The draws below stay inside these ranges and needn't reach their ends.
Inputs may be any that keep to these rules, and one draw needn't show every extreme that they name: `slot_table`: in each tick every one of the 4 slots is picked by some section.
All inputs are finite; a program needn't handle non-finite values.
Results may differ from the reference program's by a relative error of at most 0.006.
Values may be sent and summed in bfloat16 or wider, within the bound.
A program may use at most 128 MiB of HBM per device.

```python
import jax
import jax.numpy as jnp
from jax import lax

D = 4096
FF = 12288
SLOTS = 4
TOK = 256
SECTIONS = 8


def draw_slot_table(key, part):
    base = jnp.arange(SECTIONS, dtype=jnp.int32) % SLOTS
    first = jax.random.permutation(jax.random.fold_in(key, 11), base)
    second = jax.random.permutation(jax.random.fold_in(key, 23), base)
    return jnp.stack([first, second]).astype(jnp.int32)


def levels(own_key, extent, pieces, low, top_value):
    factor_of, own = 1.0, jax.random.fold_in(own_key, 6)
    for position, blocks in pieces:
        draws = jnp.exp(jax.random.uniform(jax.random.fold_in(own, position), (blocks,), jnp.float32, low / len(pieces), top_value / len(pieces)))
        factor_of = factor_of * jnp.repeat(draws, extent[position] // blocks).reshape([-1 if axis == position else 1 for axis in range(len(extent))])
    return factor_of


def normal_values(stream_key, shape, spread, bound, cuts=(), kind=jnp.bfloat16):
    values = spread * jax.random.normal(stream_key, shape, jnp.float32)
    if cuts:
        values = values * levels(stream_key, shape, cuts, -0.22, 0.18)
    return jnp.clip(values, -bound, bound).astype(kind)


def setup_inputs(seed: int = 0) -> dict:
    streams_of = jax.random.split(jax.random.key(seed), 9)
    return {
        "saved_inputs": normal_values(streams_of[0], (SECTIONS, SLOTS, TOK, D), 1.0, 6.0, ((0, 8), (2, 32))),
        "gate_weight": normal_values(streams_of[1], (SECTIONS, D, FF), D ** -0.5, 0.09375, ((0, 8), (2, 32))),
        "up_weight": normal_values(streams_of[2], (SECTIONS, D, FF), D ** -0.5, 0.09375, ((0, 8), (2, 32))),
        "down_weight": normal_values(streams_of[3], (SECTIONS, FF, D), FF ** -0.5, 0.0546875, ((0, 8), (1, 32))),
        "section_grads": normal_values(streams_of[4], (SECTIONS, TOK, D), 1.0, 6.0, ((0, 8), (1, 32))),
        "loss_grad": normal_values(streams_of[5], (TOK, D), 1.0, 6.0, ((0, 32),)),
        "trainable": jax.random.randint(streams_of[6], (1,), 0, 64 * SECTIONS).astype(jnp.int32),
        "slot_table": draw_slot_table(jax.random.fold_in(streams_of[8], 71), 0),
    }


def contract_rows(left, right):
    return lax.dot_general(left, right, (((0,), (0,)), ((), ())), preferred_element_type=jnp.float32)


def contract_cols(left, right):
    return lax.dot_general(left, right, (((1,), (1,)), ((), ())), preferred_element_type=jnp.float32)


def backward_local(inputs_full, out_full, w_gate, w_up, w_down):
    gate_pre = jnp.dot(inputs_full, w_gate, preferred_element_type=jnp.float32)
    up_pre = jnp.dot(inputs_full, w_up, preferred_element_type=jnp.float32)
    sigmoid_gate = jax.nn.sigmoid(gate_pre)
    silu_gate = gate_pre * sigmoid_gate
    hidden = (silu_gate * up_pre).astype(jnp.bfloat16)
    hidden_grad = contract_cols(out_full, w_down)
    gate_grad = (hidden_grad * up_pre * sigmoid_gate * (1.0 + gate_pre * (1.0 - sigmoid_gate))).astype(jnp.bfloat16)
    up_grad = (hidden_grad * silu_gate).astype(jnp.bfloat16)
    return hidden, gate_grad, up_grad


def section_backward(operands):
    inputs_full, out_full, w_gate, w_up, w_down = operands
    hidden, gate_grad, up_grad = backward_local(inputs_full, out_full, w_gate, w_up, w_down)
    in_grad = (contract_cols(gate_grad, w_gate) + contract_cols(up_grad, w_up)).astype(jnp.bfloat16)
    return in_grad, hidden, gate_grad, up_grad


def reference(saved_inputs, gate_weight, up_weight, down_weight, section_grads, loss_grad, trainable, slot_table):
    section_ids = jnp.arange(SECTIONS)
    inputs_one = saved_inputs[section_ids, slot_table[0]]
    first = lax.map(section_backward, (inputs_one, section_grads, gate_weight, up_weight, down_weight))
    out_two = jnp.concatenate([first[0][1:], loss_grad[None]], axis=0)
    inputs_two = saved_inputs[section_ids, slot_table[1]]
    second = lax.map(section_backward, (inputs_two, out_two, gate_weight, up_weight, down_weight))
    input_grads = jnp.stack([first[0], second[0]])
    owner = (trainable[0] % SECTIONS).astype(jnp.int32)

    def pick(stack_one, stack_two):
        return jnp.concatenate([lax.dynamic_index_in_dim(stack_one, owner, 0, keepdims=False),
                                lax.dynamic_index_in_dim(stack_two, owner, 0, keepdims=False)], axis=0)

    inputs_all = pick(inputs_one, inputs_two)
    out_all = pick(section_grads, out_two)
    hidden_all = pick(first[1], second[1])
    gate_all = pick(first[2], second[2])
    up_all = pick(first[3], second[3])
    grad_gate = contract_rows(inputs_all, gate_all).astype(jnp.bfloat16)
    grad_up = contract_rows(inputs_all, up_all).astype(jnp.bfloat16)
    grad_down = contract_rows(hidden_all, out_all).astype(jnp.bfloat16)
    return input_grads, grad_gate, grad_up, grad_down
```

```python
import functools
import heapq
import jax, jax.numpy as jnp
from jax import lax
from jax.experimental import pallas as pl
from jax.experimental.pallas import tpu as pltpu
from jax.sharding import PartitionSpec as P

MESH = pl.DeviceIdType.MESH
SIZE = {"z": 8, "x": 4}
HOP_US = 2.0
LINK_BYTES_PER_US = 50e3


class Step:
    def __init__(self, after, us=0.0, run=None, link=None, start=None, wait=None, finish=None):
        self.after, self.us, self.run = [a for a in after if a is not None], us, run
        self.link, self.start, self.wait, self.finish = link, start, wait, finish
        self.tail = 0.0


def play(steps):
    users = {s: [] for s in steps}
    for s in steps:
        for a in s.after:
            users[a].append(s)
    order = {s: i for i, s in enumerate(steps)}
    for s in reversed(steps):
        own = s.us + (HOP_US if s.link is not None else 0.0)
        s.tail = own + max([u.tail for u in users[s]], default=0.0)
    missing = {s: len(s.after) for s in steps}
    sends = [(-s.tail, order[s], s) for s in steps if missing[s] == 0 and s.link is not None]
    comps = [(-s.tail, order[s], s) for s in steps if missing[s] == 0 and s.link is None]
    heapq.heapify(sends); heapq.heapify(comps)
    arrivals, free, now, done = [], {}, 0.0, 0

    def complete(s):
        for u in users[s]:
            missing[u] -= 1
            if missing[u] == 0:
                heapq.heappush(comps if u.link is None else sends, (-u.tail, order[u], u))

    while done < len(steps):
        while sends:
            _, i, s = heapq.heappop(sends)
            s.start()
            now += 0.04
            begin = max(now, free.get(s.link, 0.0))
            free[s.link] = begin + s.us
            heapq.heappush(arrivals, (begin + s.us + HOP_US, i, s))
        if arrivals and (arrivals[0][0] <= now or not comps):
            when, _, s = heapq.heappop(arrivals)
            now = max(now, when) + 0.02
            s.wait()
            complete(s)
        elif comps:
            _, _, s = heapq.heappop(comps)
            if s.run is not None:
                s.run()
            now += s.us
            complete(s)
        else:
            raise ValueError("stuck")
        done += 1
    for s in steps:
        if s.finish is not None:
            s.finish()
    return now


def here():
    t = lax.axis_index("tensor")
    return {"z": t // 4, "x": lax.rem(t, 4)}


def moved(coord, axis, by):
    return {**coord, axis: lax.rem(coord[axis] + by % SIZE[axis], SIZE[axis])}


def tensor_id(coord):
    return {"tensor": coord["z"] * 4 + coord["x"]}


class Semaphores:
    def __init__(self, send, recv):
        self.send, self.recv, self.used = send, recv, 0

    def take(self):
        self.used += 1
        return self.send.at[self.used - 1], self.recv.at[self.used - 1]


def transfer(after, src, dst, landed, device, link, nbytes, sems):
    send, recv = sems.take()
    copy = pltpu.make_async_remote_copy(src_ref=src, dst_ref=dst, send_sem=send, recv_sem=recv,
                                        device_id=device, device_id_type=MESH)
    come = pltpu.make_async_remote_copy(src_ref=landed, dst_ref=landed, send_sem=send, recv_sem=recv,
                                        device_id=device, device_id_type=MESH)
    return Step(after, us=nbytes / LINK_BYTES_PER_US, link=link, start=copy.start, wait=come.wait_recv, finish=copy.wait_send)


def part_cols(lo, width, part):
    half = width // 256 * 128
    return {0: (lo, width), 1: (lo, half), 2: (lo + half, width - half)}[part]


def ring_hops(n):
    hops = []
    for hop in range(1, n // 2 + 1):
        whole = 2 * hop < n
        hops += [(hop, 1, 0 if whole else 1), (hop, -1, 0 if whole else 2)]
    return hops


def gather_steps(buf, rowbytes, me, first, second, lo, width, after, sems):
    steps, brought = [], {(0, 0): [after]}
    np_, nq = SIZE[first], SIZE[second]

    def add(axis, p, q, d, part, deps):
        c0, w = part_cols(lo, width, part)
        sp, sq = (p + d, q) if axis == first else (p, q + d)
        src_at = moved(moved(me, first, sp), second, sq)
        got_at = moved(moved(me, first, p), second, q)
        src = buf.at[src_at["z"], src_at["x"], ..., pl.ds(c0, w)]
        got = buf.at[got_at["z"], got_at["x"], ..., pl.ds(c0, w)]
        s = transfer(deps, src, src, got, tensor_id(moved(me, axis, d)), (axis, d), rowbytes * w, sems)
        steps.append(s)
        key = (p % np_, q % nq)
        brought.setdefault(key, []).append(s)
        return s

    for hop, d, part in ring_hops(np_):
        p = -hop * d
        add(first, p, 0, d, part, brought[((p + d) % np_, 0)])
    for p in sorted(range(np_), key=lambda o: min(o, np_ - o)):
        for hop, d, part in ring_hops(nq):
            q = -hop * d
            add(second, p, q, d, part, brought[(p, (q + d) % nq)])
    return steps, brought


def scatter_sum_steps(own, own_ready, me, first, second, lo, width, slots1, stage1, slots2, stage2, result, sems):
    n1, n2 = SIZE[first], SIZE[second]
    steps, sent1, sent2 = [], {}, {}
    f32 = jnp.float32
    half = width // 256 * 128

    def rel(part):
        c0, w = part_cols(0, width, part)
        return pl.ds(c0, w)

    def add(s):
        steps.append(s)
        return s

    qos = [n2 // 2] + [o * d for o in range(n2 // 2 - 1, 0, -1) for d in (1, -1)] + [0]
    for qo in qos:
        qi = qo % n2
        far = moved(moved(me, first, n1 // 2), second, qo)

        def put_far(far=far, qi=qi):
            stage1[qi] = own(far, lo, width).astype(stage1.dtype)
        ready = add(Step([own_ready], us=0.1, run=put_far))
        for o in range(n1 // 2, 0, -1):
            for di, d in ((0, 1), (1, -1)):
                if o == n1 // 2:
                    part = 1 if d == 1 else 2
                    src = stage1.at[qi, :, rel(part)]
                    dep = ready
                else:
                    part = 0
                    slot = slots1.at[qi, di, o]
                    prev = sent1[(qi, di, o)]
                    tgt = moved(moved(me, first, d * o), second, qo)
                    pprev = (1 if d == 1 else 2) if o + 1 == n1 // 2 else 0

                    def accumulate(slot=slot, tgt=tgt, pprev=pprev):
                        if pprev == 0:
                            slot[...] = (slot[...].astype(f32) + own(tgt, lo, width)).astype(slot.dtype)
                        else:
                            c0, w = part_cols(0, width, pprev)
                            slot[:, pl.ds(c0, w)] = (slot[:, pl.ds(c0, w)].astype(f32) + own(tgt, lo + c0, w)).astype(slot.dtype)
                            c0, w = part_cols(0, width, 3 - pprev)
                            slot[:, pl.ds(c0, w)] = own(tgt, lo + c0, w).astype(slot.dtype)
                    dep = add(Step([prev, own_ready], us=0.15, run=accumulate))
                    src = slot
                dst = slots1.at[qi, di, o - 1, :, rel(part)]
                w = part_cols(0, width, part)[1]
                sent1[(qi, di, o - 1)] = add(transfer([dep], src if part == 0 else src, dst, dst,
                    tensor_id(moved(me, first, d)), (first, d), 16 * w, sems))
    def total1(qo, c0, w):
        qi = qo % n2
        v = own(moved(me, second, qo), lo + c0, w)
        for di in (0, 1):
            if n1 // 2 > 1 or True:
                v = v + slots1[qi, di, 0, :, pl.ds(c0, w)].astype(f32)
        return v

    for o in range(n2 // 2, 0, -1):
        for di, d in ((0, 1), (1, -1)):
            qo = o * d
            qi = qo % n2
            part = (1 if d == 1 else 2) if o == n2 // 2 else 0
            c0, w = part_cols(0, width, part)
            deps = [sent1[(qi, 0, 0)], sent1[(qi, 1, 0)]]
            if o < n2 // 2:
                deps.append(sent2[(di, o)])
            pprev = 0 if o + 1 < n2 // 2 else (1 if d == 1 else 2)

            def combine(o=o, di=di, qo=qo, c0=c0, w=w, pprev=pprev):
                if o == n2 // 2:
                    stage2[di, o, :, pl.ds(c0, w)] = total1(qo, c0, w).astype(stage2.dtype)
                elif pprev == 0:
                    stage2[di, o] = (total1(qo, 0, width) + slots2[di, o].astype(f32)).astype(stage2.dtype)
                else:
                    a, b = part_cols(0, width, pprev)
                    stage2[di, o, :, pl.ds(a, b)] = (total1(qo, a, b) + slots2[di, o, :, pl.ds(a, b)].astype(f32)).astype(stage2.dtype)
                    a, b = part_cols(0, width, 3 - pprev)
                    stage2[di, o, :, pl.ds(a, b)] = total1(qo, a, b).astype(stage2.dtype)
            made = add(Step(deps, us=0.2, run=combine))
            src = stage2.at[di, o, :, pl.ds(c0, w)]
            dst = slots2.at[di, o - 1, :, pl.ds(c0, w)]
            nb = 8 * w * (4 if stage2.dtype == jnp.float32 else 2)
            sent2[(di, o - 1)] = add(transfer([made], src, dst, dst, tensor_id(moved(me, second, d)), (second, d), nb, sems))

    def last():
        v = total1(0, 0, width) + slots2[0, 0].astype(f32) + slots2[1, 0].astype(f32)
        result(lo, width, v)
    fin = add(Step([sent1[(0, 0, 0)], sent1[(0, 1, 0)], sent2[(0, 0)], sent2[(1, 0)]], us=0.2, run=last))
    return steps, fin


def shifted_2(x, axis, by):
    peers = lax.axis_size(axis)
    pairs = [(i, i + by) for i in range(peers) if 0 <= i + by < peers]
    return lax.ppermute(x, axis, pairs)


def contract_rows(left, right):
    return lax.dot_general(
        left, right, (((0,), (0,)), ((), ())), preferred_element_type=jnp.float32
    )


def contract_cols(left, right):
    return lax.dot_general(
        left, right, (((1,), (1,)), ((), ())), preferred_element_type=jnp.float32
    )


def backward_local(inputs_full, out_full, w_gate, w_up, w_down):
    gate_pre = jnp.dot(inputs_full, w_gate, preferred_element_type=jnp.float32)
    up_pre = jnp.dot(inputs_full, w_up, preferred_element_type=jnp.float32)
    sigmoid_gate = jax.nn.sigmoid(gate_pre)
    silu_gate = gate_pre * sigmoid_gate
    hidden = (silu_gate * up_pre).astype(jnp.bfloat16)
    hidden_grad = contract_cols(out_full, w_down)
    gate_grad = (
        hidden_grad * up_pre * sigmoid_gate * (1.0 + gate_pre * (1.0 - sigmoid_gate))
    ).astype(jnp.bfloat16)
    up_grad = (hidden_grad * silu_gate).astype(jnp.bfloat16)
    return (hidden, gate_grad, up_grad)


SPLITS = [("x", "z", 0, 1664), ("z", "x", 1664, 2432)]
WIDTH = 4096


def barrier(me):
    semaphore = pltpu.get_barrier_semaphore()
    for axis in "zx":
        for d in (1, -1):
            pl.semaphore_signal(semaphore, inc=1, device_id=tensor_id(moved(me, axis, d)), device_id_type=MESH)
    pl.semaphore_wait(semaphore, 4)


def gather_kernel(x_ref, buf, send, recv, local_sem):
    me = here()
    barrier(me)
    own = pltpu.make_async_copy(x_ref, buf.at[me["z"], me["x"]], local_sem)
    own.start()
    own.wait()
    sems, steps = Semaphores(send, recv), []
    for first, second, lo, width in SPLITS:
        steps += gather_steps(buf, 16 * x_ref.shape[0], me, first, second, lo, width, None, sems)[0]
    play(steps)


def gather(x, ident):
    whole = pl.BlockSpec(memory_space=pltpu.VMEM)
    return pl.pallas_call(
        gather_kernel,
        out_shape=jax.ShapeDtypeStruct((8, 4, *x.shape), x.dtype),
        in_specs=[whole],
        out_specs=whole,
        scratch_shapes=[pltpu.SemaphoreType.DMA((80,)), pltpu.SemaphoreType.DMA((80,)), pltpu.SemaphoreType.DMA],
        compiler_params=pltpu.CompilerParams(collective_id=ident, has_side_effects=True, vmem_limit_bytes=40 * 2**20),
    )(x)


def scatter_kernel(p_ref, o_ref, *rest):
    me = here()
    barrier(me)
    sems, steps = Semaphores(*rest[-2:]), []

    def own(coord, c0, w):
        return p_ref[coord["z"], coord["x"], :, pl.ds(c0, w)]

    def result(c0, w, value):
        o_ref[:, pl.ds(c0, w)] = value.astype(o_ref.dtype)

    for i, (first, second, lo, width) in enumerate(SPLITS):
        slots1, stage1, slots2, stage2 = rest[4 * i : 4 * i + 4]
        steps += scatter_sum_steps(own, None, me, first, second, lo, width, slots1, stage1, slots2, stage2, result, sems)[0]
    play(steps)


def scatter_sum(terms, ident):
    whole = pl.BlockSpec(memory_space=pltpu.VMEM)
    scratch = []
    for first, second, _, width in SPLITS:
        n1, n2 = SIZE[first], SIZE[second]
        scratch += [
            pltpu.VMEM((n2, 2, n1 // 2, 8, width), jnp.bfloat16),
            pltpu.VMEM((n2, 8, width), jnp.bfloat16),
            pltpu.VMEM((2, n2 // 2, 8, width), jnp.float32),
            pltpu.VMEM((2, n2 // 2 + 1, 8, width), jnp.float32),
        ]
    return pl.pallas_call(
        scatter_kernel,
        out_shape=jax.ShapeDtypeStruct((8, WIDTH), jnp.bfloat16),
        in_specs=[whole],
        out_specs=whole,
        scratch_shapes=scratch + [pltpu.SemaphoreType.DMA((80,)), pltpu.SemaphoreType.DMA((80,))],
        compiler_params=pltpu.CompilerParams(collective_id=ident, has_side_effects=True, vmem_limit_bytes=40 * 2**20),
    )(terms.reshape(8, 4, 8, WIDTH))


def local(
    saved_inputs,
    gate_weight,
    up_weight,
    down_weight,
    section_grads,
    loss_grad,
    trainable,
    slot_table,
):
    my_section = lax.axis_index("pipe")
    final_section = lax.axis_size("pipe") - 1
    w_gate = gate_weight[0]
    w_up = up_weight[0]
    w_down = down_weight[0]

    x0, x1 = (
        lax.dynamic_index_in_dim(saved_inputs[0], slot_table[k, my_section], 0, keepdims=False) for k in (0, 1)
    )
    early = gather(jnp.stack([x0, x1, section_grads[0]]), 0)
    x0, x1, dy0 = (early[:, :, k].reshape(256, WIDTH) for k in range(3))

    def run_tick(inputs_full, out_full, ident):
        hidden, gate_grad, up_grad = backward_local(inputs_full, out_full, w_gate, w_up, w_down)
        in_grad = scatter_sum(contract_cols(gate_grad, w_gate) + contract_cols(up_grad, w_up), ident)
        return (in_grad, inputs_full, out_full, hidden, gate_grad, up_grad)

    first = run_tick(x0, dy0, 1)
    shifted = shifted_2(first[0], "pipe", -1)
    out_second = jnp.where(my_section == final_section, loss_grad, shifted)
    dy1 = gather(out_second[None], 2)[:, :, 0].reshape(256, WIDTH)
    second = run_tick(x1, dy1, 3)
    input_grads = jnp.stack([first[0], second[0]])[:, None]
    inputs_all = jnp.concatenate([first[1], second[1]], axis=0)
    out_all = jnp.concatenate([first[2], second[2]], axis=0)
    hidden_all = jnp.concatenate([first[3], second[3]], axis=0)
    gate_all = jnp.concatenate([first[4], second[4]], axis=0)
    up_all = jnp.concatenate([first[5], second[5]], axis=0)
    owner = trainable[0] % lax.axis_size("pipe")
    is_owner = my_section == owner

    def owner_work():
        return (
            contract_rows(inputs_all, gate_all).astype(jnp.bfloat16).astype(jnp.float32),
            contract_rows(inputs_all, up_all).astype(jnp.bfloat16).astype(jnp.float32),
            contract_rows(hidden_all, out_all).astype(jnp.bfloat16).astype(jnp.float32),
        )

    def other_work():
        return (
            jnp.zeros(w_gate.shape, jnp.float32),
            jnp.zeros(w_up.shape, jnp.float32),
            jnp.zeros(w_down.shape, jnp.float32),
        )

    term_gate, term_up, term_down = lax.cond(is_owner, owner_work, other_work)
    summed_gate, summed_up = (
        lax.psum_scatter(
            term_gate.astype(jnp.bfloat16), "pipe", scatter_dimension=0, tiled=True
        ).astype(jnp.float32),
        lax.psum_scatter(
            term_up.astype(jnp.bfloat16), "pipe", scatter_dimension=0, tiled=True
        ).astype(jnp.float32),
    )
    summed_down = lax.psum_scatter(
        term_down.astype(jnp.bfloat16), "pipe", scatter_dimension=1, tiled=True
    )
    grad_gate = summed_gate.astype(jnp.bfloat16)
    grad_up = summed_up.astype(jnp.bfloat16)
    return (input_grads, grad_gate, grad_up, summed_down)


def solution(mesh):
    placed = (
        P("pipe", None, "tensor", None),
        P("pipe", None, "tensor"),
        P("pipe", None, "tensor"),
        P("pipe", "tensor", None),
        P("pipe", "tensor", None),
        P("tensor", None),
        P(),
        P(),
    )
    return jax.shard_map(
        local,
        mesh=mesh,
        in_specs=placed,
        out_specs=(
            P(None, "pipe", "tensor", None),
            P("pipe", "tensor"),
            P("pipe", "tensor"),
            P("tensor", "pipe"),
        ),
        check_vma=False,
    )
```

```python
import heapq
import jax, jax.numpy as jnp
from jax import lax
from jax.experimental import pallas as pl
from jax.experimental.pallas import tpu as pltpu
from jax.sharding import PartitionSpec as P

MESH = pl.DeviceIdType.MESH
SIZE = {"z": 8, "x": 4}
HOP_US = 2.5
LINK_BYTES_PER_US = 50e3


class Step:
    def __init__(self, after, us=0.0, run=None, link=None, start=None, wait=None, finish=None):
        self.after, self.us, self.run = [a for a in after if a is not None], us, run
        self.link, self.start, self.wait, self.finish = link, start, wait, finish
        self.tail = 0.0


def play(steps):
    users = {s: [] for s in steps}
    for s in steps:
        for a in s.after:
            users[a].append(s)
    order = {s: i for i, s in enumerate(steps)}
    for s in reversed(steps):
        own = s.us + (HOP_US if s.link is not None else 0.0)
        s.tail = own + max([u.tail for u in users[s]], default=0.0)
    missing = {s: len(s.after) for s in steps}
    sends = [(-s.tail, order[s], s) for s in steps if missing[s] == 0 and s.link is not None]
    comps = [(-s.tail, order[s], s) for s in steps if missing[s] == 0 and s.link is None]
    heapq.heapify(sends); heapq.heapify(comps)
    arrivals, free, now, done = [], {}, 0.0, 0

    def complete(s):
        for u in users[s]:
            missing[u] -= 1
            if missing[u] == 0:
                heapq.heappush(comps if u.link is None else sends, (-u.tail, order[u], u))

    while done < len(steps):
        while sends:
            _, i, s = heapq.heappop(sends)
            s.start()
            now += 0.04
            begin = max(now, free.get(s.link, 0.0))
            free[s.link] = begin + s.us
            heapq.heappush(arrivals, (begin + s.us + HOP_US, i, s))
        if arrivals and (arrivals[0][0] <= now or not comps):
            when, _, s = heapq.heappop(arrivals)
            now = max(now, when) + 0.02
            s.wait()
            complete(s)
        elif comps:
            _, _, s = heapq.heappop(comps)
            if s.run is not None:
                s.run()
            now += s.us
            complete(s)
        else:
            raise ValueError("stuck")
        done += 1
    for s in steps:
        if s.finish is not None:
            s.finish()
    return now


def here():
    t = lax.axis_index("tensor")
    return {"z": t // 4, "x": lax.rem(t, 4)}


def moved(coord, axis, by):
    return {**coord, axis: lax.rem(coord[axis] + by % SIZE[axis], SIZE[axis])}


def tensor_id(coord):
    return {"tensor": coord["z"] * 4 + coord["x"]}


class Semaphores:
    def __init__(self, send, recv):
        self.send, self.recv, self.used = send, recv, 0

    def take(self):
        self.used += 1
        return self.send.at[self.used - 1], self.recv.at[self.used - 1]


def transfer(after, src, dst, landed, device, link, nbytes, sems):
    send, recv = sems.take()
    copy = pltpu.make_async_remote_copy(src_ref=src, dst_ref=dst, send_sem=send, recv_sem=recv,
                                        device_id=device, device_id_type=MESH)
    come = pltpu.make_async_remote_copy(src_ref=landed, dst_ref=landed, send_sem=send, recv_sem=recv,
                                        device_id=device, device_id_type=MESH)
    return Step(after, us=nbytes / LINK_BYTES_PER_US, link=link, start=copy.start, wait=come.wait_recv, finish=copy.wait_send)


def part_cols(lo, width, part):
    half = width // 256 * 128
    return {0: (lo, width), 1: (lo, half), 2: (lo + half, width - half)}[part]


def ring_hops(n):
    hops = []
    for hop in range(1, n // 2 + 1):
        whole = 2 * hop < n
        hops += [(hop, 1, 0 if whole else 1), (hop, -1, 0 if whole else 2)]
    return hops


TREES = {
    "z": [(1, 0, 0), (-1, 0, 0), (2, 1, 0), (-2, -1, 0), (3, 2, 0), (-3, -2, 0), (4, 3, 1), (-4, -3, 2)],
    "x": [(1, 0, 0), (-1, 0, 0), (2, 0, 1), (-2, 0, 2)],
}


def gather_steps(buf, rowbytes, me, first, second, lo, width, after, sems, trees=TREES):
    steps, brought = [], {(0, 0): [after]}
    np_, nq = SIZE[first], SIZE[second]

    def add(axis, rp, rq, s, part, deps):
        c0, w = part_cols(lo, width, part)
        r = rp if axis == first else rq
        step = s - r
        got_at = moved(moved(me, first, -rp), second, -rq)
        src_at = moved(moved(me, first, -(s if axis == first else rp)), second, -(s if axis == second else rq))
        src = buf.at[src_at["z"], src_at["x"], ..., pl.ds(c0, w)]
        got = buf.at[got_at["z"], got_at["x"], ..., pl.ds(c0, w)]
        d = 1 if step < 0 else -1
        st = transfer(deps, src, src, got, tensor_id(moved(me, axis, -step)), (axis, d), rowbytes * w * abs(step), sems)
        steps.append(st)
        brought.setdefault((rp % np_, rq % nq), []).append(st)

    for r, s, part in trees[first]:
        add(first, r, 0, s, part, brought[(s % np_, 0)])
    for p in sorted(range(np_), key=lambda o: min(o, np_ - o)):
        for r, s, part in trees[second]:
            add(second, p, r, s, part, brought[(p, s % nq)])
    return steps, brought


def scatter_sum_steps(own, own_ready, me, first, second, lo, width, slots1, stage1, slots2, stage2, result, sems):
    n1, n2 = SIZE[first], SIZE[second]
    steps, sent1, sent2 = [], {}, {}
    f32 = jnp.float32
    half = width // 256 * 128

    def rel(part):
        c0, w = part_cols(0, width, part)
        return pl.ds(c0, w)

    def add(s):
        steps.append(s)
        return s

    qos = [n2 // 2] + [o * d for o in range(n2 // 2 - 1, 0, -1) for d in (1, -1)] + [0]
    for qo in qos:
        qi = qo % n2
        far = moved(moved(me, first, n1 // 2), second, qo)

        def put_far(far=far, qi=qi):
            stage1[qi] = own(far, lo, width).astype(stage1.dtype)
        ready = add(Step([own_ready], us=0.1, run=put_far))
        for o in range(n1 // 2, 0, -1):
            for di, d in ((0, 1), (1, -1)):
                if o == n1 // 2:
                    part = 1 if d == 1 else 2
                    src = stage1.at[qi, :, rel(part)]
                    dep = ready
                else:
                    part = 0
                    slot = slots1.at[qi, di, o]
                    prev = sent1[(qi, di, o)]
                    tgt = moved(moved(me, first, d * o), second, qo)
                    pprev = (1 if d == 1 else 2) if o + 1 == n1 // 2 else 0

                    def accumulate(slot=slot, tgt=tgt, pprev=pprev):
                        if pprev == 0:
                            slot[...] = (slot[...].astype(f32) + own(tgt, lo, width)).astype(slot.dtype)
                        else:
                            c0, w = part_cols(0, width, pprev)
                            slot[:, pl.ds(c0, w)] = (slot[:, pl.ds(c0, w)].astype(f32) + own(tgt, lo + c0, w)).astype(slot.dtype)
                            c0, w = part_cols(0, width, 3 - pprev)
                            slot[:, pl.ds(c0, w)] = own(tgt, lo + c0, w).astype(slot.dtype)
                    dep = add(Step([prev, own_ready], us=0.15, run=accumulate))
                    src = slot
                dst = slots1.at[qi, di, o - 1, :, rel(part)]
                w = part_cols(0, width, part)[1]
                sent1[(qi, di, o - 1)] = add(transfer([dep], src if part == 0 else src, dst, dst,
                    tensor_id(moved(me, first, d)), (first, d), 16 * w, sems))
    def total1(qo, c0, w):
        qi = qo % n2
        v = own(moved(me, second, qo), lo + c0, w)
        for di in (0, 1):
            if n1 // 2 > 1 or True:
                v = v + slots1[qi, di, 0, :, pl.ds(c0, w)].astype(f32)
        return v

    for o in range(n2 // 2, 0, -1):
        for di, d in ((0, 1), (1, -1)):
            qo = o * d
            qi = qo % n2
            part = (1 if d == 1 else 2) if o == n2 // 2 else 0
            c0, w = part_cols(0, width, part)
            deps = [sent1[(qi, 0, 0)], sent1[(qi, 1, 0)]]
            if o < n2 // 2:
                deps.append(sent2[(di, o)])
            pprev = 0 if o + 1 < n2 // 2 else (1 if d == 1 else 2)

            def combine(o=o, di=di, qo=qo, c0=c0, w=w, pprev=pprev):
                if o == n2 // 2:
                    stage2[di, o, :, pl.ds(c0, w)] = total1(qo, c0, w).astype(stage2.dtype)
                elif pprev == 0:
                    stage2[di, o] = (total1(qo, 0, width) + slots2[di, o].astype(f32)).astype(stage2.dtype)
                else:
                    a, b = part_cols(0, width, pprev)
                    stage2[di, o, :, pl.ds(a, b)] = (total1(qo, a, b) + slots2[di, o, :, pl.ds(a, b)].astype(f32)).astype(stage2.dtype)
                    a, b = part_cols(0, width, 3 - pprev)
                    stage2[di, o, :, pl.ds(a, b)] = total1(qo, a, b).astype(stage2.dtype)
            made = add(Step(deps, us=0.2, run=combine))
            src = stage2.at[di, o, :, pl.ds(c0, w)]
            dst = slots2.at[di, o - 1, :, pl.ds(c0, w)]
            nb = 8 * w * (4 if stage2.dtype == jnp.float32 else 2)
            sent2[(di, o - 1)] = add(transfer([made], src, dst, dst, tensor_id(moved(me, second, d)), (second, d), nb, sems))

    def last():
        v = total1(0, 0, width) + slots2[0, 0].astype(f32) + slots2[1, 0].astype(f32)
        result(lo, width, v)
    fin = add(Step([sent1[(0, 0, 0)], sent1[(0, 1, 0)], sent2[(0, 0)], sent2[(1, 0)]], us=0.2, run=last))
    return steps, fin


def contract_rows(left, right):
    return lax.dot_general(
        left, right, (((0,), (0,)), ((), ())), preferred_element_type=jnp.float32
    )


def contract_cols(left, right):
    return lax.dot_general(
        left, right, (((1,), (1,)), ((), ())), preferred_element_type=jnp.float32
    )


def backward_local(inputs_full, out_full, w_gate, w_up, w_down):
    gate_pre = jnp.dot(inputs_full, w_gate, preferred_element_type=jnp.float32)
    up_pre = jnp.dot(inputs_full, w_up, preferred_element_type=jnp.float32)
    sigmoid_gate = jax.nn.sigmoid(gate_pre)
    silu_gate = gate_pre * sigmoid_gate
    hidden = (silu_gate * up_pre).astype(jnp.bfloat16)
    hidden_grad = contract_cols(out_full, w_down)
    gate_grad = (
        hidden_grad * up_pre * sigmoid_gate * (1.0 + gate_pre * (1.0 - sigmoid_gate))
    ).astype(jnp.bfloat16)
    up_grad = (hidden_grad * silu_gate).astype(jnp.bfloat16)
    return (hidden, gate_grad, up_grad)


SPLITS = [("x", "z", 0, 1664), ("z", "x", 1664, 2432)]
SPLITS_EXT = [("x", "z", 0, 1920), ("z", "x", 1920, 2688)]
SPLITS_SMALL = [("x", "z", 0, 256), ("z", "x", 256, 256)]
WIDTH = 4096
SLICE = 512
PIPE = 8
BF16 = jnp.bfloat16
F32 = jnp.float32


def pipe_id(by):
    return {"pipe": lax.rem(lax.axis_index("pipe") + by % PIPE, PIPE)}


def place(y, core):
    return {"pipe": y * 2 + core}


def barrier(me, pipe_peers):
    semaphore = pltpu.get_barrier_semaphore()
    peers = [tensor_id(moved(me, axis, d)) for axis in "zx" for d in (1, -1)] + [tensor_id(moved(me, "x", 2))]
    if pipe_peers:
        peers += [pipe_id(k) for k in range(1, PIPE)]
    for peer in peers:
        pl.semaphore_signal(semaphore, inc=1, device_id=peer, device_id_type=MESH)
    pl.semaphore_wait(semaphore, len(peers))


def put_own(after, buf, me, value):
    def run():
        buf[me["z"], me["x"]] = value()

    return Step([after], us=0.1, run=run)


def exchange_steps(after, src, width, slots, sems, rowbytes):
    p = lax.axis_index("pipe")

    def columns(q):
        return pl.ds(pl.multiple_of(q * SLICE, SLICE), SLICE)

    def keep():
        slots[p] = src[..., columns(p)]

    steps = [Step([after], us=0.1, run=keep)]
    for k in range(1, PIPE):
        q, r = lax.rem(p + k, PIPE), lax.rem(p + PIPE - k, PIPE)
        steps.append(
            transfer([after], src.at[..., columns(q)], slots.at[p], slots.at[r], {"pipe": q}, "y" + str(k % 2), rowbytes * SLICE, sems)
        )
    return steps


def share_steps(after, owner, t_ref, out, core_in, chip_in, cand, sems):
    p = lax.axis_index("pipe")
    y, core = p // 2, lax.rem(p, 2)
    block = 96 * 384 * 2
    steps = []

    def add(step):
        steps.append(step)
        return step

    other = place(y, 1 - core)
    got = add(transfer([after], t_ref.at[:, 1 - core], core_in, core_in, other, "core", block, sems))

    def choose():
        mine = lax.rem(owner(), 2) == core
        cand[...] = jnp.where(mine, t_ref[:, core].astype(F32), core_in[...].astype(F32)).astype(BF16)
        chip_in[y] = cand[y]

    chosen = add(Step([got], us=0.3, run=choose))
    arrivals = [chosen]
    for k in (1, 2, 3):
        to, frm = lax.rem(y + k, 4), lax.rem(y + 4 - k, 4)
        arrivals.append(add(transfer([chosen], cand.at[to], chip_in.at[y], chip_in.at[frm], place(to, core), "y" + str(k % 2), 2 * block, sems)))

    def pick():
        out[y, core] = chip_in[owner() // 2]

    picked = add(Step(arrivals, us=0.1, run=pick))
    add(transfer([picked], out.at[y, core], out.at[y, core], out.at[y, 1 - core], other, "core", block / 10, sems))
    for k in (1, 2, 3):
        to, frm = lax.rem(y + k, 4), lax.rem(y + 4 - k, 4)
        come = add(transfer([picked], out.at[y, core], out.at[y, core], out.at[frm, core], place(to, core), "y" + str(k % 2), 2 * block, sems))
        add(transfer([come], out.at[frm, core], out.at[frm, core], out.at[frm, 1 - core], other, "core", block / 10, sems))
    return steps


SHARE_SCRATCH = [pltpu.VMEM((4, 96, 384), BF16), pltpu.VMEM((4, 96, 384), BF16), pltpu.VMEM((4, 96, 384), BF16)]


def sum_scratch():
    scratch = []
    for first, second, _, width in SPLITS:
        n1, n2 = SIZE[first], SIZE[second]
        scratch += [
            pltpu.VMEM((n2, 2, n1 // 2, 8, width), BF16),
            pltpu.VMEM((n2, 8, width), BF16),
            pltpu.VMEM((2, n2 // 2, 8, width), F32),
            pltpu.VMEM((2, n2 // 2 + 1, 8, width), F32),
        ]
    return scratch


def sum_steps(p_ref, o_ref, me, scratch, sems):
    def own(coord, c0, w):
        return p_ref[coord["z"], coord["x"], :, pl.ds(c0, w)]

    def result(c0, w, value):
        o_ref[:, pl.ds(c0, w)] = value.astype(o_ref.dtype)

    steps, last = [], []
    for i, (first, second, lo, width) in enumerate(SPLITS):
        more, end = scatter_sum_steps(own, None, me, first, second, lo, width, *scratch[4 * i : 4 * i + 4], result, sems)
        steps += more
        last.append(end)
    return steps, last


def gather_all(buf, rowbytes, me, splits, after, sems):
    steps = []
    for first, second, lo, width in splits:
        steps += gather_steps(buf, rowbytes, me, first, second, lo, width, after, sems)[0]
    return steps


def call(kernel, ident, ins, outs, scratch, count, smem=0):
    whole = pl.BlockSpec(memory_space=pltpu.VMEM)
    return pl.pallas_call(
        kernel,
        out_shape=[jax.ShapeDtypeStruct(shape, BF16) for shape in outs],
        in_specs=[pl.BlockSpec(memory_space=pltpu.SMEM)] * smem + [whole] * (len(ins) - smem),
        out_specs=[whole] * len(outs),
        scratch_shapes=scratch + [pltpu.SemaphoreType.DMA((count,)), pltpu.SemaphoreType.DMA((count,))],
        compiler_params=pltpu.CompilerParams(collective_id=ident, has_side_effects=True, vmem_limit_bytes=48 * 2**20),
    )(*ins)


def first_kernel(x_ref, buf, send, recv):
    me = here()
    barrier(me, False)
    sems = Semaphores(send, recv)
    own = put_own(None, buf, me, lambda: x_ref[...])
    play([own] + gather_all(buf, 32, me, SPLITS, own, sems))


def middle_kernel(owner_ref, p_ref, rows_ref, loss_ref, t_ref, ig_ref, x1_buf, ext_buf, dy_buf, t_out, ext_in, ext1_in, shift_in, *rest):
    me = here()
    barrier(me, True)
    sems = Semaphores(*rest[-2:])
    p = lax.axis_index("pipe")
    owner = lambda: owner_ref[0]

    steps, ends = sum_steps(p_ref, ig_ref, me, rest[3:-2], sems)

    shift = transfer(ends, ig_ref, shift_in, shift_in, pipe_id(-1), "y1", 8 * WIDTH * 4, sems)
    steps.append(shift)
    spread = exchange_steps(None, ig_ref, WIDTH, ext1_in, sems, 16)
    for s in spread:
        s.after = list(ends)
    steps += spread

    def next_rows():
        dy_buf[me["z"], me["x"], :, pl.ds(0, WIDTH)] = jnp.where(
            p == PIPE - 1, loss_ref[...].astype(F32), shift_in[...].astype(F32)
        ).astype(BF16)
        nearest = ext1_in[lax.rem(owner() + 1, PIPE)].astype(F32)
        mine = loss_ref[:, pl.ds(pl.multiple_of(p * SLICE, SLICE), SLICE)].astype(F32)
        dy_buf[me["z"], me["x"], :, pl.ds(WIDTH, SLICE)] = jnp.where(owner() == PIPE - 1, mine, nearest).astype(BF16)

    ready = Step([shift] + spread, us=0.2, run=next_rows)
    steps.append(ready)
    steps += gather_all(dy_buf, 16, me, SPLITS_EXT, ready, sems)

    own = put_own(None, x1_buf, me, lambda: rows_ref[1])
    steps.append(own)
    steps += gather_all(x1_buf, 16, me, SPLITS, own, sems)

    early = exchange_steps(None, rows_ref, WIDTH, ext_in, sems, 48)
    steps += early
    owned = Step(early, us=0.1, run=lambda: ext_buf.__setitem__((me["z"], me["x"]), ext_in[owner()]))
    steps.append(owned)
    steps += gather_all(ext_buf, 48, me, SPLITS_SMALL, owned, sems)
    steps += share_steps(None, owner, t_ref, t_out, *rest[:3], sems)
    play(steps)


def last_kernel(owner_ref, p_ref, t_ref, ig_ref, t_out, *rest):
    me = here()
    barrier(me, True)
    sems = Semaphores(*rest[-2:])
    steps, _ = sum_steps(p_ref, ig_ref, me, rest[3:-2], sems)
    steps += share_steps(None, lambda: owner_ref[0], t_ref, t_out, *rest[:3], sems)
    play(steps)


def local(
    saved_inputs,
    gate_weight,
    up_weight,
    down_weight,
    section_grads,
    loss_grad,
    trainable,
    slot_table,
):
    my_section = lax.axis_index("pipe")
    w_gate = gate_weight[0]
    w_up = up_weight[0]
    w_down = down_weight[0]
    owner = lax.rem(lax.rem(trainable, PIPE) + PIPE, PIPE)
    x0, x1 = (
        lax.dynamic_index_in_dim(saved_inputs[0], slot_table[k, my_section], 0, keepdims=False) for k in (0, 1)
    )
    dy0 = section_grads[0]
    (early,) = call(first_kernel, 0, (jnp.stack([x0, dy0]),), [(8, 4, 2, 8, WIDTH)], [], 80)
    x0_full, dy0_full = (early[:, :, k].reshape(256, WIDTH) for k in range(2))

    def run_tick(inputs_full, out_full):
        parts = backward_local(inputs_full, out_full, w_gate, w_up, w_down)
        terms = contract_cols(parts[1], w_gate) + contract_cols(parts[2], w_up)
        return terms.reshape(8, 4, 8, WIDTH), jnp.stack(parts).reshape(4, 2, 96, 384)

    terms, parts0 = run_tick(x0_full, dy0_full)
    ig0, x1_buf, ext, dy1_buf, parts0 = call(
        middle_kernel,
        1,
        (owner, terms, jnp.stack([x0, x1, dy0]), loss_grad, parts0),
        [(8, WIDTH), (8, 4, 8, WIDTH), (8, 4, 3, 8, SLICE), (8, 4, 8, WIDTH + SLICE), (4, 2, 96, 384)],
        [pltpu.VMEM((PIPE, 3, 8, SLICE), BF16), pltpu.VMEM((PIPE, 8, SLICE), BF16), pltpu.VMEM((8, WIDTH), BF16)]
        + SHARE_SCRATCH
        + sum_scratch(),
        400,
        smem=1,
    )
    dy1_all = dy1_buf.reshape(256, WIDTH + SLICE)
    terms, parts1 = run_tick(x1_buf.reshape(256, WIDTH), dy1_all[:, :WIDTH])
    ig1, parts1 = call(
        last_kernel,
        2,
        (owner, terms, parts1),
        [(8, WIDTH), (4, 2, 96, 384)],
        SHARE_SCRATCH + sum_scratch(),
        100,
        smem=1,
    )
    input_grads = jnp.stack([ig0, ig1])[:, None]
    hidden, gate, up = jnp.concatenate([parts0.reshape(3, 256, 384), parts1.reshape(3, 256, 384)], axis=1)
    ext_x0, ext_x1, ext_dy0 = (ext[:, :, k].reshape(256, SLICE) for k in range(3))
    inputs_all = jnp.concatenate([ext_x0, ext_x1], axis=0)
    out_all = jnp.concatenate([ext_dy0, dy1_all[:, WIDTH:]], axis=0)
    return (
        input_grads,
        contract_rows(inputs_all, gate).astype(BF16),
        contract_rows(inputs_all, up).astype(BF16),
        contract_rows(hidden, out_all).astype(BF16),
    )


def solution(mesh):
    placed = (
        P("pipe", None, "tensor", None),
        P("pipe", None, "tensor"),
        P("pipe", None, "tensor"),
        P("pipe", "tensor", None),
        P("pipe", "tensor", None),
        P("tensor", None),
        P(),
        P(),
    )
    return jax.shard_map(
        local,
        mesh=mesh,
        in_specs=placed,
        out_specs=(
            P(None, "pipe", "tensor", None),
            P("pipe", "tensor"),
            P("pipe", "tensor"),
            P("tensor", "pipe"),
        ),
        check_vma=False,
    )
```

```python
import heapq
import jax, jax.numpy as jnp
from jax import lax
from jax.experimental import pallas as pl
from jax.experimental.pallas import tpu as pltpu
from jax.sharding import PartitionSpec as P

MESH = pl.DeviceIdType.MESH
SIZE = {"z": 8, "x": 4}
HOP_US = 2.5
LINK_BYTES_PER_US = 50e3


class Step:
    def __init__(self, after, us=0.0, run=None, link=None, start=None, wait=None, finish=None):
        self.after, self.us, self.run = [a for a in after if a is not None], us, run
        self.link, self.start, self.wait, self.finish = link, start, wait, finish
        self.tail = 0.0


def play(steps):
    users = {s: [] for s in steps}
    for s in steps:
        for a in s.after:
            users[a].append(s)
    order = {s: i for i, s in enumerate(steps)}
    for s in reversed(steps):
        own = s.us + (HOP_US if s.link is not None else 0.0)
        s.tail = own + max([u.tail for u in users[s]], default=0.0)
    missing = {s: len(s.after) for s in steps}
    sends = [(-s.tail, order[s], s) for s in steps if missing[s] == 0 and s.link is not None]
    comps = [(-s.tail, order[s], s) for s in steps if missing[s] == 0 and s.link is None]
    heapq.heapify(sends); heapq.heapify(comps)
    arrivals, free, now, done = [], {}, 0.0, 0

    def complete(s):
        for u in users[s]:
            missing[u] -= 1
            if missing[u] == 0:
                heapq.heappush(comps if u.link is None else sends, (-u.tail, order[u], u))

    while done < len(steps):
        while sends:
            _, i, s = heapq.heappop(sends)
            s.start()
            now += 0.04
            begin = max(now, free.get(s.link, 0.0))
            free[s.link] = begin + s.us
            heapq.heappush(arrivals, (begin + s.us + HOP_US, i, s))
        if arrivals and (arrivals[0][0] <= now or not comps):
            when, _, s = heapq.heappop(arrivals)
            now = max(now, when) + 0.02
            if s.wait is not None:
                s.wait()
            complete(s)
        elif comps:
            _, _, s = heapq.heappop(comps)
            if s.run is not None:
                s.run()
            now += s.us
            complete(s)
        else:
            raise ValueError("stuck")
        done += 1
    for s in steps:
        if s.finish is not None:
            s.finish()
    return now


def here():
    t = lax.axis_index("tensor")
    return {"z": t // 4, "x": lax.rem(t, 4)}


def moved(coord, axis, by):
    return {**coord, axis: lax.rem(coord[axis] + by % SIZE[axis], SIZE[axis])}


def tensor_id(coord):
    return {"tensor": coord["z"] * 4 + coord["x"]}


class Semaphores:
    def __init__(self, send, recv, counts=None, recv_used=0):
        self.send, self.recv = send, recv
        self.counts = [0] if counts is None else counts
        self.recv_used = recv_used

    def again(self, recv_used):
        return Semaphores(self.send, self.recv, self.counts, recv_used)

    def to_send(self):
        self.counts[0] += 1
        if self.counts[0] > self.send.shape[0]:
            raise ValueError("too few")
        return self.send.at[self.counts[0] - 1]

    def to_recv(self):
        self.recv_used += 1
        if self.recv_used > self.recv.shape[0]:
            raise ValueError("too few")
        return self.recv.at[self.recv_used - 1]


def transfer(after, src, dst, landed, device, link, nbytes, sems, send=None, recv=None):
    own_send, own_recv = send is None, recv is None
    send = sems.to_send() if own_send else send
    recv = sems.to_recv() if own_recv else recv
    copy = pltpu.make_async_remote_copy(src_ref=src, dst_ref=dst, send_sem=send, recv_sem=recv,
                                        device_id=device, device_id_type=MESH)
    come = pltpu.make_async_remote_copy(src_ref=landed, dst_ref=landed, send_sem=send, recv_sem=recv,
                                        device_id=device, device_id_type=MESH)
    return Step(after, us=nbytes / LINK_BYTES_PER_US, link=link, start=copy.start,
                wait=come.wait_recv if own_recv else None, finish=copy.wait_send if own_send else None)


def all_of(ref, sem):
    return pltpu.make_async_copy(ref, ref, sem).wait


def part_cols(lo, width, part):
    half = width // 256 * 128
    return {0: (lo, width), 1: (lo, half), 2: (lo + half, width - half)}[part]


def ring_hops(n):
    hops = []
    for hop in range(1, n // 2 + 1):
        whole = 2 * hop < n
        hops += [(hop, 1, 0 if whole else 1), (hop, -1, 0 if whole else 2)]
    return hops


TREES = {
    "z": [(1, 0, 0), (-1, 0, 0), (2, 1, 0), (-2, -1, 0), (3, 2, 0), (-3, -2, 0), (4, 3, 1), (-4, -3, 2)],
    "x": [(1, 0, 0), (-1, 0, 0), (2, 0, 1), (-2, 0, 2)],
}


def gather_steps(place_of, rowbytes, me, first, second, lo, width, after, sems, trees=TREES):
    steps, brought, leaves, leaf_parts = [], {(0, 0): [after]}, [], 0
    np_, nq = SIZE[first], SIZE[second]
    send, leaf = sems.to_send(), sems.to_recv()
    senders = {x % nq for _, x, _ in trees[second]}

    def slab(coord, c0, w):
        return place_of(coord["z"] * 4 + coord["x"], None, c0, w)

    def add(axis, rp, rq, s, part, deps, is_leaf):
        c0, w = part_cols(lo, width, part)
        r = rp if axis == first else rq
        step = s - r
        got_at = moved(moved(me, first, -rp), second, -rq)
        src_at = moved(moved(me, first, -(s if axis == first else rp)), second, -(s if axis == second else rq))
        src, got = slab(src_at, c0, w), slab(got_at, c0, w)
        d = 1 if step < 0 else -1
        st = transfer(deps, src, src, got, tensor_id(moved(me, axis, -step)), (axis, d), rowbytes * w * abs(step), sems,
                      send=send, recv=leaf if is_leaf else None)
        steps.append(st)
        if is_leaf:
            leaves.append(st)
        brought.setdefault((rp % np_, rq % nq), []).append(st)

    for r, s, part in trees[first]:
        add(first, r, 0, s, part, brought[(s % np_, 0)], False)
    for p in sorted(range(np_), key=lambda o: min(o, np_ - o)):
        for r, s, part in trees[second]:
            is_leaf = r % nq not in senders
            add(second, p, r, s, part, brought[(p, s % nq)], is_leaf)
            leaf_parts += (2 if part == 0 else 1) * is_leaf
    steps.append(Step(leaves, us=0.02, run=all_of(place_of(0, leaf_parts // 2, lo, width), leaf)))
    steps[0].finish = all_of(place_of(0, np_ * nq - 1, lo, width), send)
    return steps


def scatter_sum_steps(own, own_ready, me, first, second, lo, width, slots1, stage1, slots2, stage2, result, sems):
    n1, n2 = SIZE[first], SIZE[second]
    steps, sent1, sent2 = [], {}, {}
    send1, send2 = sems.to_send(), sems.to_send()

    def at1(qi, di, o):
        return (qi * 2 + di) * (n1 // 2) + o

    def at2(di, o):
        return di * (n2 // 2) + o

    f32 = jnp.float32
    half = width // 256 * 128

    def rel(part):
        c0, w = part_cols(0, width, part)
        return pl.ds(c0, w)

    def add(s):
        steps.append(s)
        return s

    qos = [n2 // 2] + [o * d for o in range(n2 // 2 - 1, 0, -1) for d in (1, -1)] + [0]
    for qo in qos:
        qi = qo % n2
        far = moved(moved(me, first, n1 // 2), second, qo)

        def put_far(far=far, qi=qi):
            stage1[qi] = own(far, lo, width).astype(stage1.dtype)
        ready = add(Step([own_ready], us=0.1, run=put_far))
        for o in range(n1 // 2, 0, -1):
            for di, d in ((0, 1), (1, -1)):
                if o == n1 // 2:
                    part = 1 if d == 1 else 2
                    src = stage1.at[qi, :, rel(part)]
                    dep = ready
                else:
                    part = 0
                    slot = slots1.at[at1(qi, di, o)]
                    prev = sent1[(qi, di, o)]
                    tgt = moved(moved(me, first, d * o), second, qo)
                    pprev = (1 if d == 1 else 2) if o + 1 == n1 // 2 else 0

                    def accumulate(slot=slot, tgt=tgt, pprev=pprev):
                        if pprev == 0:
                            slot[...] = (slot[...].astype(f32) + own(tgt, lo, width)).astype(slot.dtype)
                        else:
                            c0, w = part_cols(0, width, pprev)
                            slot[:, pl.ds(c0, w)] = (slot[:, pl.ds(c0, w)].astype(f32) + own(tgt, lo + c0, w)).astype(slot.dtype)
                            c0, w = part_cols(0, width, 3 - pprev)
                            slot[:, pl.ds(c0, w)] = own(tgt, lo + c0, w).astype(slot.dtype)
                    dep = add(Step([prev, own_ready], us=0.15, run=accumulate))
                    src = slot
                dst = slots1.at[at1(qi, di, o - 1), :, rel(part)]
                w = part_cols(0, width, part)[1]
                sent1[(qi, di, o - 1)] = add(transfer([dep], src if part == 0 else src, dst, dst,
                    tensor_id(moved(me, first, d)), (first, d), 16 * w, sems, send=send1))
    def total1(qo, c0, w):
        qi = qo % n2
        v = own(moved(me, second, qo), lo + c0, w)
        for di in (0, 1):
            if n1 // 2 > 1 or True:
                v = v + slots1[at1(qi, di, 0), :, pl.ds(c0, w)].astype(f32)
        return v

    for o in range(n2 // 2, 0, -1):
        for di, d in ((0, 1), (1, -1)):
            qo = o * d
            qi = qo % n2
            part = (1 if d == 1 else 2) if o == n2 // 2 else 0
            c0, w = part_cols(0, width, part)
            deps = [sent1[(qi, 0, 0)], sent1[(qi, 1, 0)]]
            if o < n2 // 2:
                deps.append(sent2[(di, o)])
            pprev = 0 if o + 1 < n2 // 2 else (1 if d == 1 else 2)

            def combine(o=o, di=di, qo=qo, c0=c0, w=w, pprev=pprev):
                if o == n2 // 2:
                    stage2[di, o, :, pl.ds(c0, w)] = total1(qo, c0, w).astype(stage2.dtype)
                elif pprev == 0:
                    stage2[di, o] = (total1(qo, 0, width) + slots2[at2(di, o)].astype(f32)).astype(stage2.dtype)
                else:
                    a, b = part_cols(0, width, pprev)
                    stage2[di, o, :, pl.ds(a, b)] = (total1(qo, a, b) + slots2[at2(di, o), :, pl.ds(a, b)].astype(f32)).astype(stage2.dtype)
                    a, b = part_cols(0, width, 3 - pprev)
                    stage2[di, o, :, pl.ds(a, b)] = total1(qo, a, b).astype(stage2.dtype)
            made = add(Step(deps, us=0.2, run=combine))
            src = stage2.at[di, o, :, pl.ds(c0, w)]
            dst = slots2.at[at2(di, o - 1), :, pl.ds(c0, w)]
            nb = 8 * w * (4 if stage2.dtype == jnp.float32 else 2)
            sent2[(di, o - 1)] = add(transfer([made], src, dst, dst, tensor_id(moved(me, second, d)), (second, d), nb, sems, send=send2))

    def last():
        v = total1(0, 0, width) + slots2[at2(0, 0)].astype(f32) + slots2[at2(1, 0)].astype(f32)
        result(lo, width, v)
    fin = add(Step([sent1[(0, 0, 0)], sent1[(0, 1, 0)], sent2[(0, 0)], sent2[(1, 0)]], us=0.2, run=last,
                   finish=lambda: (all_of(slots1.at[pl.ds(0, n2 * (n1 - 1))], send1)(), all_of(slots2.at[pl.ds(0, n2 - 1)], send2)())))
    return steps, fin


def contract_rows(left, right):
    return lax.dot_general(
        left, right, (((0,), (0,)), ((), ())), preferred_element_type=jnp.float32
    )


def contract_cols(left, right):
    return lax.dot_general(
        left, right, (((1,), (1,)), ((), ())), preferred_element_type=jnp.float32
    )


SPLITS = [("x", "z", 0, 1664), ("z", "x", 1664, 2432)]
SPLITS_SMALL = [("z", "x", 0, 512)]
WIDTH = 4096
SLICE = 512
PIPE = 8
BF16 = jnp.bfloat16
F32 = jnp.float32


def pipe_id(by):
    return {"pipe": lax.rem(lax.axis_index("pipe") + by % PIPE, PIPE)}


def place(y, core):
    return {"pipe": y * 2 + core}


def barrier(me, pipe_peers):
    semaphore = pltpu.get_barrier_semaphore()
    peers = [tensor_id(moved(me, axis, d)) for axis in "zx" for d in (1, -1)] + [tensor_id(moved(me, "x", 2))]
    if pipe_peers:
        peers += [pipe_id(k) for k in range(1, PIPE)]
    for peer in peers:
        pl.semaphore_signal(semaphore, inc=1, device_id=peer, device_id_type=MESH)
    pl.semaphore_wait(semaphore, len(peers))


def exchange_steps(after, src, width, slots, sems, rowbytes):
    p = lax.axis_index("pipe")

    def columns(q):
        return pl.ds(pl.multiple_of(q * SLICE, SLICE), SLICE)

    def keep():
        slots[p] = src[..., columns(p)]

    steps = [Step([after], us=0.1, run=keep)]
    send, recv, sent = sems.to_send(), sems.to_recv(), []
    for k in range(1, PIPE):
        q, r = lax.rem(p + k, PIPE), lax.rem(p + PIPE - k, PIPE)
        sent.append(transfer([after], src.at[..., columns(q)], slots.at[p], slots.at[r], {"pipe": q}, "y" + str(k % 2),
                             rowbytes * SLICE, sems, send=send, recv=recv))
    every = slots.at[pl.ds(0, PIPE - 1)]
    sent[0].finish = all_of(every, send)
    return steps + sent + [Step(sent, us=0.02, run=all_of(every, recv))]


def share_steps(after, owner, t_ref, out, tick, core_in, chip_in, cand, sems):
    p = lax.axis_index("pipe")
    y, core = p // 2, lax.rem(p, 2)
    block = 96 * 384 * 2
    steps = []

    def add(step):
        steps.append(step)
        return step

    other = place(y, 1 - core)
    got = add(transfer([after], t_ref.at[:, :, 1 - core], core_in, core_in, other, "core", block / 3, sems))

    def choose():
        mine = lax.rem(owner(), 2) == core
        for j in range(4):
            cand[j] = jnp.where(mine, t_ref[:, j, core].astype(F32), core_in[:, j].astype(F32)).astype(BF16)
        chip_in[y] = cand[y]

    chosen = add(Step([got], us=0.3, run=choose))
    arrivals = [chosen]
    for k in (1, 2, 3):
        to, frm = lax.rem(y + k, 4), lax.rem(y + 4 - k, 4)
        arrivals.append(add(transfer([chosen], cand.at[to], chip_in.at[y], chip_in.at[frm], place(to, core), "y" + str(k), (2 if k == 2 else 1) * block, sems)))

    def pick():
        out[:, tick, y, core] = chip_in[owner() // 2]

    picked = add(Step(arrivals, us=0.1, run=pick))
    mine = out.at[:, tick, y, core]
    add(transfer([picked], mine, mine, out.at[:, tick, y, 1 - core], other, "core", block / 10, sems))
    for k in (1, 2, 3):
        to, frm = lax.rem(y + k, 4), lax.rem(y + 4 - k, 4)
        theirs = out.at[:, tick, frm, core]
        come = add(transfer([picked], mine, mine, theirs, place(to, core), "y" + str(k), (2 if k == 2 else 1) * block, sems))
        add(transfer([come], theirs, theirs, out.at[:, tick, frm, 1 - core], other, "core", block / 10, sems))
    return steps


SHARE_SCRATCH = [pltpu.VMEM((3, 4, 32, 384), BF16), pltpu.VMEM((4, 3, 32, 384), BF16), pltpu.VMEM((4, 3, 32, 384), BF16)]


def sum_scratch():
    scratch = []
    for first, second, _, width in SPLITS:
        n1, n2 = SIZE[first], SIZE[second]
        scratch += [
            pltpu.VMEM((n2 * 2 * (n1 // 2), 8, width), BF16),
            pltpu.VMEM((n2, 8, width), BF16),
            pltpu.VMEM((n2, 8, width), F32),
            pltpu.VMEM((2, n2 // 2 + 1, 8, width), F32),
        ]
    return scratch


def sum_steps(p_ref, o_ref, tick, me, ready, scratch, sems):
    def own(coord, c0, w):
        return p_ref[coord["z"], coord["x"], :, pl.ds(c0, w)]

    def result(c0, w, value):
        o_ref[tick, :, pl.ds(c0, w)] = value.astype(o_ref.dtype)

    steps, last = [], []
    for i, (first, second, lo, width) in enumerate(SPLITS):
        more, end = scatter_sum_steps(own, ready[i], me, first, second, lo, width, *scratch[4 * i : 4 * i + 4], result, sems)
        steps += more
        last.append(end)
    return steps, last


def gather_all(slab, rowbytes, me, splits, after, sems):
    steps, by_split = [], []
    for first, second, lo, width in splits:
        more = gather_steps(slab, rowbytes, me, first, second, lo, width, after, sems)
        steps += more
        by_split.append(more)
    return steps, by_split


def slabs(buf):
    return lambda i, n, c0, w: buf.at[i if n is None else pl.ds(i, n), :, pl.ds(c0, w)]


KC = 1024
NC = 512


def rows_of(buf, c0, w):
    return buf[:, :, pl.ds(c0, w)].astype(F32).reshape(256, w).astype(BF16)


def needs(by_split, c0, w):
    out = []
    for (_, _, lo, width), steps in zip(SPLITS, by_split):
        if lo < c0 + w and c0 < lo + width:
            out += steps
    return out


def chain(buf, by_split, own, once, product, acc, us):
    steps, last = [], []
    for i in range(WIDTH // KC):

        def run(i=i):
            if i == 0:
                once()
                acc[...] = product(rows_of(buf, 0, KC), 0)
            else:
                acc[...] += product(rows_of(buf, i * KC, KC), i * KC)

        step = Step([own] + needs(by_split, i * KC, KC) + last, us=us, run=run)
        last = [step]
        steps.append(step)
    return steps, step


def kernel(
    trainable_ref, slot_ref, saved_ref, section_ref, loss_ref, gate_hbm, up_hbm, down_hbm,
    ig_ref, gate_ref, up_ref, down_ref,
    exts, shared, w_in, w_down, x0_buf, x1_buf, dy0_buf, dy1_buf, terms, acc0, acc1, acc_h, grads, t0, t1, rows,
    ext_in, ext1_in, shift_in, w_sem, *rest,
):
    me = here()
    p = lax.axis_index("pipe")
    loads = [
        pltpu.make_async_copy(gate_hbm, w_in.at[:, pl.ds(0, 384)], w_sem.at[0]),
        pltpu.make_async_copy(up_hbm, w_in.at[:, pl.ds(384, 384)], w_sem.at[1]),
        pltpu.make_async_copy(down_hbm, w_down, w_sem.at[2]),
    ]
    for load in loads:
        load.start()
    rows[0] = saved_ref[slot_ref[0, p]]
    rows[1] = saved_ref[slot_ref[1, p]]
    rows[2] = section_ref[...]
    for buf, k in ((x0_buf, 0), (x1_buf, 1), (dy0_buf, 2)):
        buf[me["z"] * 4 + me["x"]] = rows[k]
    barrier(me, True)
    sems = Semaphores(*rest[-2:])
    scratch = rest[:-2]
    owner = lambda: lax.rem(lax.rem(trainable_ref[0], PIPE) + PIPE, PIPE)
    steps = []

    def add(more):
        steps.extend(more)

    begin = Step([], us=0.0)
    add([begin])

    def in_product(a, c0):
        return jnp.dot(a, w_in[pl.ds(c0, KC), :], preferred_element_type=F32)

    def down_product(a, c0):
        return contract_cols(a, w_down[:, pl.ds(c0, KC)])

    def wait_in():
        loads[0].wait()
        loads[1].wait()

    def nothing():
        return None

    x0_from = sems.recv_used
    more, x0_parts = gather_all(slabs(x0_buf), 16, me, SPLITS, begin, sems)
    add(more)
    more, dy0_parts = gather_all(slabs(dy0_buf), 16, me, SPLITS, begin, sems)
    add(more)

    def tick(k, x_buf, x_parts, dy_buf, dy_parts, dy_own, acc, t_ref, share, sums, sum_sems):
        more, up_end = chain(x_buf, x_parts, begin, wait_in if k == 0 else nothing, in_product, acc, 0.7)
        add(more)
        more, down_end = chain(dy_buf, dy_parts, dy_own, loads[2].wait if k == 0 else nothing, down_product, acc_h, 0.5)
        add(more)
        halves = []
        for b in range(8):

            def run(b=b):
                at = pl.ds(b * 32, 32)
                gate, up, hidden_grad = acc[at, pl.ds(0, 384)], acc[at, pl.ds(384, 384)], acc_h[at, :]
                sigmoid_gate = jax.nn.sigmoid(gate)
                silu_gate = gate * sigmoid_gate
                gate_grad = (hidden_grad * up * sigmoid_gate * (1.0 + gate * (1.0 - sigmoid_gate))).astype(BF16)
                up_grad = (hidden_grad * silu_gate).astype(BF16)
                t_ref[0, b // 2, b % 2] = (silu_gate * up).astype(BF16)
                t_ref[1, b // 2, b % 2] = gate_grad
                t_ref[2, b // 2, b % 2] = up_grad
                grads[at, pl.ds(0, 384)] = gate_grad
                grads[at, pl.ds(384, 384)] = up_grad

            halves.append(Step([up_end, down_end], us=0.15, run=run))
        add(halves)
        made = []
        for b in range(WIDTH // NC):

            def run(b=b):
                value = contract_cols(grads[...], w_in[pl.ds(b * NC, NC), :])
                terms[:, :, :, pl.ds(b * NC, NC)] = value.reshape(8, 4, 8, NC)

            made.append(Step(halves, us=0.35, run=run))
        add(made)
        ready = []
        for _, _, lo, width in SPLITS:
            ready.append(Step([m for b, m in enumerate(made) if lo < (b + 1) * NC and b * NC < lo + width]))
        add(ready)
        more, ends = sum_steps(terms, ig_ref, k, me, ready, sums, sum_sems)
        add(more)
        shared_from = Step(halves)
        add([shared_from])
        more = share_steps(shared_from, owner, t_ref, shared, k, *share, sems)
        add(more)
        return ends, more

    n = len(SHARE_SCRATCH)
    m = 4 * len(SPLITS)
    sum_from = sems.recv_used
    ends, shares0 = tick(0, x0_buf, x0_parts, dy0_buf, dy0_parts, begin, acc0, t0, scratch[:n], scratch[2 * n : 2 * n + m], sems)

    shift = transfer(ends, ig_ref.at[0], shift_in, shift_in, pipe_id(-1), "y1", 8 * WIDTH, sems)

    def next_rows():
        dy1_buf[me["z"] * 4 + me["x"]] = jnp.where(p == PIPE - 1, loss_ref[...].astype(F32), shift_in[...].astype(F32)).astype(BF16)

    dy1_own = Step([shift], us=0.1, run=next_rows)
    add([shift, dy1_own])
    more, dy1_parts = gather_all(slabs(dy1_buf), 16, me, SPLITS, dy1_own, sems.again(x0_from))
    add(more)
    x1_begin = Step(x0_parts[0])
    add([x1_begin])
    more, x1_parts = gather_all(slabs(x1_buf), 16, me, SPLITS, x1_begin, sems)
    add(more)

    both = Step(ends)
    spread = exchange_steps(both, ig_ref.at[0], WIDTH, ext1_in, sems, 16)

    def next_slice():
        nearest = ext1_in[lax.rem(owner() + 1, PIPE)].astype(F32)
        mine = loss_ref[:, pl.ds(pl.multiple_of(p * SLICE, SLICE), SLICE)].astype(F32)
        exts[3, me["z"] * 4 + me["x"]] = jnp.where(owner() == PIPE - 1, mine, nearest).astype(BF16)

    sliced = Step(spread, us=0.1, run=next_slice)
    add([both] + spread + [sliced])
    dy_slices = (gather_all(lambda i, n, c0, w: exts.at[3, i if n is None else pl.ds(i, n), :, pl.ds(c0, w)], 16, me, SPLITS_SMALL, sliced, sems)[0])
    add(dy_slices)

    early = exchange_steps(begin, rows, WIDTH, ext_in, sems, 48)

    def first_slices():
        exts[pl.ds(0, 3), me["z"] * 4 + me["x"]] = ext_in[owner()]

    owned = Step(early + sum(dy1_parts, []), us=0.1, run=first_slices)
    add(early + [owned])
    x_slices = (gather_all(lambda i, n, c0, w: exts.at[pl.ds(0, 3), i if n is None else pl.ds(i, n), :, pl.ds(c0, w)], 48, me, SPLITS_SMALL, owned, sems)[0])
    add(x_slices)

    _, shares1 = tick(
        1, x1_buf, x1_parts, dy1_buf, dy1_parts, dy1_own, acc1, t1, scratch[n : 2 * n], scratch[2 * n + m :], sems.again(sum_from)
    )

    def stacked(k):
        return exts[pl.ds(k, 2)].astype(F32).reshape(512, SLICE).astype(BF16)

    def part(k):
        return shared[k].reshape(512, 384)

    def gate_out():
        gate_ref[...] = contract_rows(stacked(0), part(1)).astype(BF16)

    def up_out():
        up_ref[...] = contract_rows(stacked(0), part(2)).astype(BF16)

    def down_out():
        down_ref[...] = contract_rows(part(0), stacked(2)).astype(BF16)

    add([Step(shares0 + shares1 + x_slices, us=1.0, run=gate_out), Step(shares0 + shares1 + x_slices, us=1.0, run=up_out)])
    add([Step(shares0 + shares1 + x_slices + dy_slices, us=1.0, run=down_out)])
    play(in_order(steps))


def in_order(steps):
    out, seen = [], set()

    def visit(s):
        if s not in seen:
            seen.add(s)
            for a in s.after:
                visit(a)
            out.append(s)

    for s in steps:
        visit(s)
    return out


def place_out(*refs):
    for source, target in zip(refs[:4], refs[4:]):
        target[...] = source[...]


SENDS, RECVS = 44, 240


def local(
    saved_inputs,
    gate_weight,
    up_weight,
    down_weight,
    section_grads,
    loss_grad,
    trainable,
    slot_table,
):
    vmem = pl.BlockSpec(memory_space=pltpu.VMEM)
    smem = pl.BlockSpec(memory_space=pltpu.SMEM)
    hbm = pl.BlockSpec(memory_space=pl.ANY)
    rows = pltpu.VMEM((32, 8, WIDTH), BF16)
    ig, gate, up, down = pl.pallas_call(
        kernel,
        out_shape=[
            jax.ShapeDtypeStruct(shape, BF16)
            for shape in ((2, 8, WIDTH), (SLICE, 384), (SLICE, 384), (384, SLICE))
        ],
        in_specs=[smem, smem, vmem, vmem, vmem, hbm, hbm, hbm],
        out_specs=[vmem] * 4,
        scratch_shapes=[
            pltpu.VMEM((4, 32, 8, SLICE), BF16),
            pltpu.VMEM((3, 2, 4, 2, 32, 384), BF16),
            pltpu.VMEM((WIDTH, 768), BF16),
            pltpu.VMEM((384, WIDTH), BF16),
            rows, rows, rows, rows,
            pltpu.VMEM((8, 4, 8, WIDTH), F32),
            pltpu.VMEM((256, 768), F32),
            pltpu.VMEM((256, 768), F32),
            pltpu.VMEM((256, 384), F32),
            pltpu.VMEM((256, 768), BF16),
            pltpu.VMEM((3, 4, 2, 32, 384), BF16),
            pltpu.VMEM((3, 4, 2, 32, 384), BF16),
            pltpu.VMEM((3, 8, WIDTH), BF16),
            pltpu.VMEM((PIPE, 3, 8, SLICE), BF16),
            pltpu.VMEM((PIPE, 8, SLICE), BF16),
            pltpu.VMEM((8, WIDTH), BF16),
            pltpu.SemaphoreType.DMA((3,)),
            *SHARE_SCRATCH,
            *SHARE_SCRATCH,
            *sum_scratch(),
            *sum_scratch(),
            pltpu.SemaphoreType.DMA((SENDS,)),
            pltpu.SemaphoreType.DMA((RECVS,)),
        ],
        compiler_params=pltpu.CompilerParams(collective_id=0, has_side_effects=True, vmem_limit_bytes=58 * 2**20),
        cost_estimate=pl.CostEstimate(flops=8 * 10**9, bytes_accessed=12 * 10**6, transcendentals=2 * 10**5),
    )(trainable, slot_table, saved_inputs[0], section_grads[0], loss_grad, gate_weight[0], up_weight[0], down_weight[0])
    return pl.pallas_call(
        place_out,
        out_shape=[jax.ShapeDtypeStruct(a.shape, a.dtype) for a in (ig[:, None], gate, up, down)],
        in_specs=[vmem] * 4,
        out_specs=[vmem] * 4,
    )(ig[:, None], gate, up, down)


def solution(mesh):
    placed = (
        P("pipe", None, "tensor", None),
        P("pipe", None, "tensor"),
        P("pipe", None, "tensor"),
        P("pipe", "tensor", None),
        P("pipe", "tensor", None),
        P("tensor", None),
        P(),
        P(),
    )
    return jax.shard_map(
        local,
        mesh=mesh,
        in_specs=placed,
        out_specs=(
            P(None, "pipe", "tensor", None),
            P("pipe", "tensor"),
            P("pipe", "tensor"),
            P("tensor", "pipe"),
        ),
        check_vma=False,
    )
```

```python
import heapq
import jax, jax.numpy as jnp
from jax import lax
from jax.experimental import pallas as pl
from jax.experimental.pallas import tpu as pltpu
from jax.sharding import PartitionSpec as P

MESH = pl.DeviceIdType.MESH
SIZE = {"z": 8, "x": 4}
HOP_US = 2.5
LINK_BYTES_PER_US = 50e3


class Step:
    def __init__(self, after, us=0.0, run=None, link=None, start=None, wait=None, finish=None):
        self.after, self.us, self.run = [a for a in after if a is not None], us, run
        self.link, self.start, self.wait, self.finish = link, start, wait, finish
        self.tail = 0.0


def play(steps):
    users = {s: [] for s in steps}
    for s in steps:
        for a in s.after:
            users[a].append(s)
    order = {s: i for i, s in enumerate(steps)}
    for s in reversed(steps):
        own = s.us + (HOP_US if s.link is not None else 0.0)
        s.tail = own + max([u.tail for u in users[s]], default=0.0)
    missing = {s: len(s.after) for s in steps}
    sends = [(-s.tail, order[s], s) for s in steps if missing[s] == 0 and s.link is not None]
    comps = [(-s.tail, order[s], s) for s in steps if missing[s] == 0 and s.link is None]
    heapq.heapify(sends); heapq.heapify(comps)
    arrivals, free, now, done = [], {}, 0.0, 0

    def complete(s):
        for u in users[s]:
            missing[u] -= 1
            if missing[u] == 0:
                heapq.heappush(comps if u.link is None else sends, (-u.tail, order[u], u))

    while done < len(steps):
        while sends:
            _, i, s = heapq.heappop(sends)
            s.start()
            now += 0.04
            begin = max(now, free.get(s.link, 0.0))
            free[s.link] = begin + s.us
            heapq.heappush(arrivals, (begin + s.us + HOP_US, i, s))
        if arrivals and (arrivals[0][0] <= now or not comps):
            when, _, s = heapq.heappop(arrivals)
            now = max(now, when) + 0.02
            if s.wait is not None:
                s.wait()
            complete(s)
        elif comps:
            _, _, s = heapq.heappop(comps)
            if s.run is not None:
                s.run()
            now += s.us
            complete(s)
        else:
            raise ValueError("stuck")
        done += 1
    for s in steps:
        if s.finish is not None:
            s.finish()
    return now


def here():
    t = lax.axis_index("tensor")
    return {"z": t // 4, "x": lax.rem(t, 4)}


def moved(coord, axis, by):
    return {**coord, axis: lax.rem(coord[axis] + by % SIZE[axis], SIZE[axis])}


def tensor_id(coord):
    return {"tensor": coord["z"] * 4 + coord["x"]}


class Semaphores:
    def __init__(self, send, recv, counts=None, recv_used=0):
        self.send, self.recv = send, recv
        self.counts = [0] if counts is None else counts
        self.recv_used = recv_used

    def again(self, recv_used):
        return Semaphores(self.send, self.recv, self.counts, recv_used)

    def to_send(self):
        self.counts[0] += 1
        if self.counts[0] > self.send.shape[0]:
            raise ValueError("too few")
        return self.send.at[self.counts[0] - 1]

    def to_recv(self):
        self.recv_used += 1
        if self.recv_used > self.recv.shape[0]:
            raise ValueError("too few")
        return self.recv.at[self.recv_used - 1]


def transfer(after, src, dst, landed, device, link, nbytes, sems, send=None, recv=None):
    own_send, own_recv = send is None, recv is None
    send = sems.to_send() if own_send else send
    recv = sems.to_recv() if own_recv else recv
    copy = pltpu.make_async_remote_copy(src_ref=src, dst_ref=dst, send_sem=send, recv_sem=recv,
                                        device_id=device, device_id_type=MESH)
    come = pltpu.make_async_remote_copy(src_ref=landed, dst_ref=landed, send_sem=send, recv_sem=recv,
                                        device_id=device, device_id_type=MESH)
    return Step(after, us=nbytes / LINK_BYTES_PER_US, link=link, start=copy.start,
                wait=come.wait_recv if own_recv else None, finish=copy.wait_send if own_send else None)


def all_of(ref, sem):
    return pltpu.make_async_copy(ref, ref, sem).wait


def part_cols(lo, width, part):
    half = width // 256 * 128
    return {0: (lo, width), 1: (lo, half), 2: (lo + half, width - half)}[part]


def ring_hops(n):
    hops = []
    for hop in range(1, n // 2 + 1):
        whole = 2 * hop < n
        hops += [(hop, 1, 0 if whole else 1), (hop, -1, 0 if whole else 2)]
    return hops


TREES = {
    "z": [(1, 0, 0), (-1, 0, 0), (2, 1, 0), (-2, -1, 0), (3, 2, 0), (-3, -2, 0), (4, 3, 1), (-4, -3, 2)],
    "x": [(1, 0, 0), (-1, 0, 0), (2, 0, 1), (-2, 0, 2)],
}


def gather_steps(place_of, rowbytes, me, first, second, lo, width, after, sems, trees=TREES):
    steps, brought, leaves, leaf_parts = [], {(0, 0): [after]}, [], 0
    np_, nq = SIZE[first], SIZE[second]
    send, leaf = sems.to_send(), sems.to_recv()
    senders = {x % nq for _, x, _ in trees[second]}

    def slab(coord, c0, w):
        return place_of(coord["z"] * 4 + coord["x"], None, c0, w)

    def add(axis, rp, rq, s, part, deps, is_leaf):
        c0, w = part_cols(lo, width, part)
        r = rp if axis == first else rq
        step = s - r
        got_at = moved(moved(me, first, -rp), second, -rq)
        src_at = moved(moved(me, first, -(s if axis == first else rp)), second, -(s if axis == second else rq))
        src, got = slab(src_at, c0, w), slab(got_at, c0, w)
        d = 1 if step < 0 else -1
        st = transfer(deps, src, src, got, tensor_id(moved(me, axis, -step)), (axis, d), rowbytes * w * abs(step), sems,
                      send=send, recv=leaf if is_leaf else None)
        steps.append(st)
        if is_leaf:
            leaves.append(st)
        brought.setdefault((rp % np_, rq % nq), []).append(st)

    for r, s, part in trees[first]:
        add(first, r, 0, s, part, brought[(s % np_, 0)], False)
    for p in sorted(range(np_), key=lambda o: min(o, np_ - o)):
        for r, s, part in trees[second]:
            is_leaf = r % nq not in senders
            add(second, p, r, s, part, brought[(p, s % nq)], is_leaf)
            leaf_parts += (2 if part == 0 else 1) * is_leaf
    steps.append(Step(leaves, us=0.02, run=all_of(place_of(0, leaf_parts // 2, lo, width), leaf)))
    steps[0].finish = all_of(place_of(0, np_ * nq - 1, lo, width), send)
    return steps


def scatter_sum_steps(own, own_ready, me, first, second, lo, width, slots1, stage1, slots2, stage2, result, sems):
    n1, n2 = SIZE[first], SIZE[second]
    steps, sent1, sent2 = [], {}, {}
    send1, send2 = sems.to_send(), sems.to_send()

    def at1(qi, di, o):
        return (qi * 2 + di) * (n1 // 2) + o

    def at2(di, o):
        return di * (n2 // 2) + o

    f32 = jnp.float32
    half = width // 256 * 128

    def rel(part):
        c0, w = part_cols(0, width, part)
        return pl.ds(c0, w)

    def add(s):
        steps.append(s)
        return s

    qos = [n2 // 2] + [o * d for o in range(n2 // 2 - 1, 0, -1) for d in (1, -1)] + [0]
    for qo in qos:
        qi = qo % n2
        far = moved(moved(me, first, n1 // 2), second, qo)

        def put_far(far=far, qi=qi):
            stage1[qi] = own(far, lo, width).astype(stage1.dtype)
        ready = add(Step([own_ready], us=0.1, run=put_far))
        for o in range(n1 // 2, 0, -1):
            for di, d in ((0, 1), (1, -1)):
                if o == n1 // 2:
                    part = 1 if d == 1 else 2
                    src = stage1.at[qi, :, rel(part)]
                    dep = ready
                else:
                    part = 0
                    slot = slots1.at[at1(qi, di, o)]
                    prev = sent1[(qi, di, o)]
                    tgt = moved(moved(me, first, d * o), second, qo)
                    pprev = (1 if d == 1 else 2) if o + 1 == n1 // 2 else 0

                    def accumulate(slot=slot, tgt=tgt, pprev=pprev):
                        if pprev == 0:
                            slot[...] = (slot[...].astype(f32) + own(tgt, lo, width)).astype(slot.dtype)
                        else:
                            c0, w = part_cols(0, width, pprev)
                            slot[:, pl.ds(c0, w)] = (slot[:, pl.ds(c0, w)].astype(f32) + own(tgt, lo + c0, w)).astype(slot.dtype)
                            c0, w = part_cols(0, width, 3 - pprev)
                            slot[:, pl.ds(c0, w)] = own(tgt, lo + c0, w).astype(slot.dtype)
                    dep = add(Step([prev, own_ready], us=0.15, run=accumulate))
                    src = slot
                dst = slots1.at[at1(qi, di, o - 1), :, rel(part)]
                w = part_cols(0, width, part)[1]
                sent1[(qi, di, o - 1)] = add(transfer([dep], src if part == 0 else src, dst, dst,
                    tensor_id(moved(me, first, d)), (first, d), 16 * w, sems, send=send1))
    def total1(qo, c0, w):
        qi = qo % n2
        v = own(moved(me, second, qo), lo + c0, w)
        for di in (0, 1):
            if n1 // 2 > 1 or True:
                v = v + slots1[at1(qi, di, 0), :, pl.ds(c0, w)].astype(f32)
        return v

    for o in range(n2 // 2, 0, -1):
        for di, d in ((0, 1), (1, -1)):
            qo = o * d
            qi = qo % n2
            part = (1 if d == 1 else 2) if o == n2 // 2 else 0
            c0, w = part_cols(0, width, part)
            deps = [sent1[(qi, 0, 0)], sent1[(qi, 1, 0)]]
            if o < n2 // 2:
                deps.append(sent2[(di, o)])
            pprev = 0 if o + 1 < n2 // 2 else (1 if d == 1 else 2)

            def combine(o=o, di=di, qo=qo, c0=c0, w=w, pprev=pprev):
                if o == n2 // 2:
                    stage2[di, o, :, pl.ds(c0, w)] = total1(qo, c0, w).astype(stage2.dtype)
                elif pprev == 0:
                    stage2[di, o] = (total1(qo, 0, width) + slots2[at2(di, o)].astype(f32)).astype(stage2.dtype)
                else:
                    a, b = part_cols(0, width, pprev)
                    stage2[di, o, :, pl.ds(a, b)] = (total1(qo, a, b) + slots2[at2(di, o), :, pl.ds(a, b)].astype(f32)).astype(stage2.dtype)
                    a, b = part_cols(0, width, 3 - pprev)
                    stage2[di, o, :, pl.ds(a, b)] = total1(qo, a, b).astype(stage2.dtype)
            made = add(Step(deps, us=0.2, run=combine))
            src = stage2.at[di, o, :, pl.ds(c0, w)]
            dst = slots2.at[at2(di, o - 1), :, pl.ds(c0, w)]
            nb = 8 * w * (4 if stage2.dtype == jnp.float32 else 2)
            sent2[(di, o - 1)] = add(transfer([made], src, dst, dst, tensor_id(moved(me, second, d)), (second, d), nb, sems, send=send2))

    def last():
        v = total1(0, 0, width) + slots2[at2(0, 0)].astype(f32) + slots2[at2(1, 0)].astype(f32)
        result(lo, width, v)
    fin = add(Step([sent1[(0, 0, 0)], sent1[(0, 1, 0)], sent2[(0, 0)], sent2[(1, 0)]], us=0.2, run=last,
                   finish=lambda: (all_of(slots1.at[pl.ds(0, n2 * (n1 - 1))], send1)(), all_of(slots2.at[pl.ds(0, n2 - 1)], send2)())))
    return steps, fin


def contract_rows(left, right):
    return lax.dot_general(
        left, right, (((0,), (0,)), ((), ())), preferred_element_type=jnp.float32
    )


def contract_cols(left, right):
    return lax.dot_general(
        left, right, (((1,), (1,)), ((), ())), preferred_element_type=jnp.float32
    )


SPLITS = [("x", "z", 0, 1664), ("z", "x", 1664, 2432)]
SUM_SPLITS = [("x", "z", 0, 2816), ("z", "x", 2816, 1280)]
SPLITS_SMALL = [("z", "x", 0, 512)]
WIDTH = 4096
SLICE = 512
PIPE = 8
BF16 = jnp.bfloat16
F32 = jnp.float32


def pipe_id(by):
    return {"pipe": lax.rem(lax.axis_index("pipe") + by % PIPE, PIPE)}


def place(y, core):
    return {"pipe": y * 2 + core}


def barrier(me, pipe_peers):
    semaphore = pltpu.get_barrier_semaphore()
    peers = [tensor_id(moved(me, axis, d)) for axis in "zx" for d in (1, -1)] + [tensor_id(moved(me, "x", 2))]
    if pipe_peers:
        peers += [pipe_id(k) for k in range(1, PIPE)]
    for peer in peers:
        pl.semaphore_signal(semaphore, inc=1, device_id=peer, device_id_type=MESH)
    pl.semaphore_wait(semaphore, len(peers))


def exchange_steps(after, src, width, slots, sems, rowbytes):
    p = lax.axis_index("pipe")

    def columns(q):
        return pl.ds(pl.multiple_of(q * SLICE, SLICE), SLICE)

    def keep():
        slots[p] = src[..., columns(p)]

    steps = [Step([after], us=0.1, run=keep)]
    send, recv, sent = sems.to_send(), sems.to_recv(), []
    for k in range(1, PIPE):
        q, r = lax.rem(p + k, PIPE), lax.rem(p + PIPE - k, PIPE)
        sent.append(transfer([after], src.at[..., columns(q)], slots.at[p], slots.at[r], {"pipe": q}, "y" + str(k % 2),
                             rowbytes * SLICE, sems, send=send, recv=recv))
    every = slots.at[pl.ds(0, PIPE - 1)]
    sent[0].finish = all_of(every, send)
    return steps + sent + [Step(sent, us=0.02, run=all_of(every, recv))]


def share_steps(after, owner, t_ref, out, tick, core_in, chip_in, cand, sems):
    p = lax.axis_index("pipe")
    y, core = p // 2, lax.rem(p, 2)
    block = 96 * 384 * 2
    steps = []

    def add(step):
        steps.append(step)
        return step

    other = place(y, 1 - core)
    got = add(transfer([after], t_ref.at[:, :, 1 - core], core_in, core_in, other, "core", block / 3, sems))

    def choose():
        mine = lax.rem(owner(), 2) == core
        for j in range(4):
            cand[j] = jnp.where(mine, t_ref[:, j, core].astype(F32), core_in[:, j].astype(F32)).astype(BF16)
        chip_in[y] = cand[y]

    chosen = add(Step([got], us=0.3, run=choose))
    arrivals = [chosen]
    for k in (1, 2, 3):
        to, frm = lax.rem(y + k, 4), lax.rem(y + 4 - k, 4)
        arrivals.append(add(transfer([chosen], cand.at[to], chip_in.at[y], chip_in.at[frm], place(to, core), "y" + str(k), (2 if k == 2 else 1) * block, sems)))

    def pick():
        out[:, tick, y, core] = chip_in[owner() // 2]

    picked = add(Step(arrivals, us=0.1, run=pick))
    mine = out.at[:, tick, y, core]
    add(transfer([picked], mine, mine, out.at[:, tick, y, 1 - core], other, "core", block / 10, sems))
    for k in (1, 2, 3):
        to, frm = lax.rem(y + k, 4), lax.rem(y + 4 - k, 4)
        theirs = out.at[:, tick, frm, core]
        come = add(transfer([picked], mine, mine, theirs, place(to, core), "y" + str(k), (2 if k == 2 else 1) * block, sems))
        add(transfer([come], theirs, theirs, out.at[:, tick, frm, 1 - core], other, "core", block / 10, sems))
    return steps


SHARE_SCRATCH = [pltpu.VMEM((3, 4, 32, 384), BF16), pltpu.VMEM((4, 3, 32, 384), BF16), pltpu.VMEM((4, 3, 32, 384), BF16)]


def sum_scratch():
    scratch = []
    for first, second, _, width in SUM_SPLITS:
        n1, n2 = SIZE[first], SIZE[second]
        scratch += [
            pltpu.VMEM((n2 * 2 * (n1 // 2), 8, width), BF16),
            pltpu.VMEM((n2, 8, width), BF16),
            pltpu.VMEM((n2, 8, width), F32),
            pltpu.VMEM((2, n2 // 2 + 1, 8, width), F32),
        ]
    return scratch


def sum_steps(p_ref, o_ref, tick, me, ready, scratch, sems):
    def own(coord, c0, w):
        return p_ref[coord["z"], coord["x"], :, pl.ds(c0, w)]

    def result(c0, w, value):
        o_ref[tick, :, pl.ds(c0, w)] = value.astype(o_ref.dtype)

    steps, last = [], []
    for i, (first, second, lo, width) in enumerate(SUM_SPLITS):
        more, end = scatter_sum_steps(own, ready[i], me, first, second, lo, width, *scratch[4 * i : 4 * i + 4], result, sems)
        steps += more
        last.append(end)
    return steps, last


def gather_all(slab, rowbytes, me, splits, after, sems):
    steps, by_split = [], []
    for first, second, lo, width in splits:
        more = gather_steps(slab, rowbytes, me, first, second, lo, width, after, sems)
        steps += more
        by_split.append(more)
    return steps, by_split


def slabs(buf):
    return lambda i, n, c0, w: buf.at[i if n is None else pl.ds(i, n), :, pl.ds(c0, w)]


KC = 1024
NC = 512


def rows_of(buf, c0, w):
    return buf[:, :, pl.ds(c0, w)].astype(F32).reshape(256, w).astype(BF16)


def needs(by_split, c0, w):
    out = []
    for (_, _, lo, width), steps in zip(SPLITS, by_split):
        if lo < c0 + w and c0 < lo + width:
            out += steps
    return out


def chain(buf, by_split, own, once, product, acc, us):
    steps, last = [], []
    for i in range(WIDTH // KC):

        def run(i=i):
            if i == 0:
                once()
                acc[...] = product(rows_of(buf, 0, KC), 0)
            else:
                acc[...] += product(rows_of(buf, i * KC, KC), i * KC)

        step = Step([own] + needs(by_split, i * KC, KC) + last, us=us, run=run)
        last = [step]
        steps.append(step)
    return steps, step


def kernel(
    trainable_ref, slot_ref, saved_ref, section_ref, loss_ref, gate_hbm, up_hbm, down_hbm,
    ig_ref, gate_ref, up_ref, down_ref,
    exts, shared, w_in, w_down, x0_buf, x1_buf, dy0_buf, dy1_buf, terms, acc0, acc1, acc_h, grads, t0, t1, rows,
    ext_in, ext1_in, shift_in, w_sem, *rest,
):
    me = here()
    p = lax.axis_index("pipe")
    loads = [
        pltpu.make_async_copy(gate_hbm, w_in.at[:, pl.ds(0, 384)], w_sem.at[0]),
        pltpu.make_async_copy(up_hbm, w_in.at[:, pl.ds(384, 384)], w_sem.at[1]),
        pltpu.make_async_copy(down_hbm, w_down, w_sem.at[2]),
    ]
    for load in loads:
        load.start()
    rows[0] = saved_ref[slot_ref[0, p]]
    rows[1] = saved_ref[slot_ref[1, p]]
    rows[2] = section_ref[...]
    for buf, k in ((x0_buf, 0), (x1_buf, 1), (dy0_buf, 2)):
        buf[me["z"] * 4 + me["x"]] = rows[k]
    barrier(me, True)
    sems = Semaphores(*rest[-2:])
    scratch = rest[:-2]
    owner = lambda: lax.rem(lax.rem(trainable_ref[0], PIPE) + PIPE, PIPE)
    steps = []

    def add(more):
        steps.extend(more)

    begin = Step([], us=0.0)
    add([begin])

    def in_product(a, c0):
        return jnp.dot(a, w_in[pl.ds(c0, KC), :], preferred_element_type=F32)

    def down_product(a, c0):
        return contract_cols(a, w_down[:, pl.ds(c0, KC)])

    def wait_in():
        loads[0].wait()
        loads[1].wait()

    def nothing():
        return None

    x0_from = sems.recv_used
    more, x0_parts = gather_all(slabs(x0_buf), 16, me, SPLITS, begin, sems)
    add(more)
    more, dy0_parts = gather_all(slabs(dy0_buf), 16, me, SPLITS, begin, sems)
    add(more)

    def tick(k, x_buf, x_parts, dy_buf, dy_parts, dy_own, acc, t_ref, share, sums, sum_sems):
        more, up_end = chain(x_buf, x_parts, begin, wait_in if k == 0 else nothing, in_product, acc, 0.7)
        add(more)
        more, down_end = chain(dy_buf, dy_parts, dy_own, loads[2].wait if k == 0 else nothing, down_product, acc_h, 0.5)
        add(more)
        halves = []
        for b in range(8):

            def run(b=b):
                at = pl.ds(b * 32, 32)
                gate, up, hidden_grad = acc[at, pl.ds(0, 384)], acc[at, pl.ds(384, 384)], acc_h[at, :]
                sigmoid_gate = jax.nn.sigmoid(gate)
                silu_gate = gate * sigmoid_gate
                gate_grad = (hidden_grad * up * sigmoid_gate * (1.0 + gate * (1.0 - sigmoid_gate))).astype(BF16)
                up_grad = (hidden_grad * silu_gate).astype(BF16)
                t_ref[0, b // 2, b % 2] = (silu_gate * up).astype(BF16)
                t_ref[1, b // 2, b % 2] = gate_grad
                t_ref[2, b // 2, b % 2] = up_grad
                grads[at, pl.ds(0, 384)] = gate_grad
                grads[at, pl.ds(384, 384)] = up_grad

            halves.append(Step([up_end, down_end], us=0.15, run=run))
        add(halves)
        made = []
        for b in range(WIDTH // NC):

            def run(b=b):
                value = contract_cols(grads[...], w_in[pl.ds(b * NC, NC), :])
                terms[:, :, :, pl.ds(b * NC, NC)] = value.reshape(8, 4, 8, NC)

            made.append(Step(halves, us=0.35, run=run))
        add(made)
        ready = []
        for _, _, lo, width in SUM_SPLITS:
            ready.append(Step([m for b, m in enumerate(made) if lo < (b + 1) * NC and b * NC < lo + width]))
        add(ready)
        more, ends = sum_steps(terms, ig_ref, k, me, ready, sums, sum_sems)
        add(more)
        shared_from = Step(halves)
        add([shared_from])
        more = share_steps(shared_from, owner, t_ref, shared, k, *share, sems)
        add(more)
        return ends, more

    n = len(SHARE_SCRATCH)
    m = 4 * len(SUM_SPLITS)
    sum_from = sems.recv_used
    ends, shares0 = tick(0, x0_buf, x0_parts, dy0_buf, dy0_parts, begin, acc0, t0, scratch[:n], scratch[2 * n : 2 * n + m], sems)

    shift = transfer(ends, ig_ref.at[0], shift_in, shift_in, pipe_id(-1), "y1", 8 * WIDTH, sems)

    def next_rows():
        dy1_buf[me["z"] * 4 + me["x"]] = jnp.where(p == PIPE - 1, loss_ref[...].astype(F32), shift_in[...].astype(F32)).astype(BF16)

    dy1_own = Step([shift], us=0.1, run=next_rows)
    add([shift, dy1_own])
    more, dy1_parts = gather_all(slabs(dy1_buf), 16, me, SPLITS, dy1_own, sems.again(x0_from))
    add(more)
    x1_begin = Step(x0_parts[0])
    add([x1_begin])
    more, x1_parts = gather_all(slabs(x1_buf), 16, me, SPLITS, x1_begin, sems)
    add(more)

    both = Step(ends)
    spread = exchange_steps(both, ig_ref.at[0], WIDTH, ext1_in, sems, 16)

    def next_slice():
        nearest = ext1_in[lax.rem(owner() + 1, PIPE)].astype(F32)
        mine = loss_ref[:, pl.ds(pl.multiple_of(p * SLICE, SLICE), SLICE)].astype(F32)
        exts[3, me["z"] * 4 + me["x"]] = jnp.where(owner() == PIPE - 1, mine, nearest).astype(BF16)

    sliced = Step(spread, us=0.1, run=next_slice)
    add([both] + spread + [sliced])
    dy_slices = (gather_all(lambda i, n, c0, w: exts.at[3, i if n is None else pl.ds(i, n), :, pl.ds(c0, w)], 16, me, SPLITS_SMALL, sliced, sems)[0])
    add(dy_slices)

    early = exchange_steps(begin, rows, WIDTH, ext_in, sems, 48)

    def first_slices():
        exts[pl.ds(0, 3), me["z"] * 4 + me["x"]] = ext_in[owner()]

    owned = Step(early + sum(dy1_parts, []), us=0.1, run=first_slices)
    add(early + [owned])
    x_slices = (gather_all(lambda i, n, c0, w: exts.at[pl.ds(0, 3), i if n is None else pl.ds(i, n), :, pl.ds(c0, w)], 48, me, SPLITS_SMALL, owned, sems)[0])
    add(x_slices)

    _, shares1 = tick(
        1, x1_buf, x1_parts, dy1_buf, dy1_parts, dy1_own, acc1, t1, scratch[n : 2 * n], scratch[2 * n + m :], sems.again(sum_from)
    )

    def stacked(k):
        return exts[pl.ds(k, 2)].astype(F32).reshape(512, SLICE).astype(BF16)

    def part(k):
        return shared[k].reshape(512, 384)

    def gate_out():
        gate_ref[...] = contract_rows(stacked(0), part(1)).astype(BF16)

    def up_out():
        up_ref[...] = contract_rows(stacked(0), part(2)).astype(BF16)

    def down_out():
        down_ref[...] = contract_rows(part(0), stacked(2)).astype(BF16)

    add([Step(shares0 + shares1 + x_slices, us=1.0, run=gate_out), Step(shares0 + shares1 + x_slices, us=1.0, run=up_out)])
    add([Step(shares0 + shares1 + x_slices + dy_slices, us=1.0, run=down_out)])
    play(in_order(steps))


def in_order(steps):
    out, seen = [], set()

    def visit(s):
        if s not in seen:
            seen.add(s)
            for a in s.after:
                visit(a)
            out.append(s)

    for s in steps:
        visit(s)
    return out


def place_out(*refs):
    for source, target in zip(refs[:4], refs[4:]):
        target[...] = source[...]


SENDS, RECVS = 44, 240


def local(
    saved_inputs,
    gate_weight,
    up_weight,
    down_weight,
    section_grads,
    loss_grad,
    trainable,
    slot_table,
):
    vmem = pl.BlockSpec(memory_space=pltpu.VMEM)
    smem = pl.BlockSpec(memory_space=pltpu.SMEM)
    hbm = pl.BlockSpec(memory_space=pl.ANY)
    rows = pltpu.VMEM((32, 8, WIDTH), BF16)
    ig, gate, up, down = pl.pallas_call(
        kernel,
        out_shape=[
            jax.ShapeDtypeStruct(shape, BF16)
            for shape in ((2, 8, WIDTH), (SLICE, 384), (SLICE, 384), (384, SLICE))
        ],
        in_specs=[smem, smem, vmem, vmem, vmem, hbm, hbm, hbm],
        out_specs=[vmem] * 4,
        scratch_shapes=[
            pltpu.VMEM((4, 32, 8, SLICE), BF16),
            pltpu.VMEM((3, 2, 4, 2, 32, 384), BF16),
            pltpu.VMEM((WIDTH, 768), BF16),
            pltpu.VMEM((384, WIDTH), BF16),
            rows, rows, rows, rows,
            pltpu.VMEM((8, 4, 8, WIDTH), F32),
            pltpu.VMEM((256, 768), F32),
            pltpu.VMEM((256, 768), F32),
            pltpu.VMEM((256, 384), F32),
            pltpu.VMEM((256, 768), BF16),
            pltpu.VMEM((3, 4, 2, 32, 384), BF16),
            pltpu.VMEM((3, 4, 2, 32, 384), BF16),
            pltpu.VMEM((3, 8, WIDTH), BF16),
            pltpu.VMEM((PIPE, 3, 8, SLICE), BF16),
            pltpu.VMEM((PIPE, 8, SLICE), BF16),
            pltpu.VMEM((8, WIDTH), BF16),
            pltpu.SemaphoreType.DMA((3,)),
            *SHARE_SCRATCH,
            *SHARE_SCRATCH,
            *sum_scratch(),
            *sum_scratch(),
            pltpu.SemaphoreType.DMA((SENDS,)),
            pltpu.SemaphoreType.DMA((RECVS,)),
        ],
        compiler_params=pltpu.CompilerParams(collective_id=0, has_side_effects=True, vmem_limit_bytes=58 * 2**20),
        cost_estimate=pl.CostEstimate(flops=8 * 10**9, bytes_accessed=12 * 10**6, transcendentals=2 * 10**5),
    )(trainable, slot_table, saved_inputs[0], section_grads[0], loss_grad, gate_weight[0], up_weight[0], down_weight[0])
    return pl.pallas_call(
        place_out,
        out_shape=[jax.ShapeDtypeStruct(a.shape, a.dtype) for a in (ig[:, None], gate, up, down)],
        in_specs=[vmem] * 4,
        out_specs=[vmem] * 4,
    )(ig[:, None], gate, up, down)


def solution(mesh):
    placed = (
        P("pipe", None, "tensor", None),
        P("pipe", None, "tensor"),
        P("pipe", None, "tensor"),
        P("pipe", "tensor", None),
        P("pipe", "tensor", None),
        P("tensor", None),
        P(),
        P(),
    )
    return jax.shard_map(
        local,
        mesh=mesh,
        in_specs=placed,
        out_specs=(
            P(None, "pipe", "tensor", None),
            P("pipe", "tensor"),
            P("pipe", "tensor"),
            P("tensor", "pipe"),
        ),
        check_vma=False,
    )
```
